512 devices in a mesh: sub: 32 (over x_lo, z), beam: 16 (over x_hi, y, core).
Axes of the slice: x: 4 (x_hi: 2, x_lo: 2; x = x_hi * 2 + x_lo), y: 4, z: 16, core: 2. Of those that a mesh axis runs over, the one named last changes fastest.
Arguments:
- echoes: bfloat16 [64, 32, 2, 16384], P('sub', 'beam'), may hold values from -6 to 6
- matched_filter: float32 [2, 16384], replicated, may hold values from -6 to 6
- steering: bfloat16 [2, 128, 32], P(None, 'beam'), may hold values from -1 to 1
- kernels: bfloat16 [4, 2, 2, 128, 128], replicated, may hold values from -0.375 to 0.375
- blend_gains: float32 [4, 2, 2, 2], replicated, may hold values from 0.3 to 1
- beam_taps: int32 [4, 2, 2, 128], P(None, None, None, 'beam'), may hold values from -1 to 0
Outputs:
- polar_image: bfloat16 [64, 128, 2, 16384], P('sub', 'beam')
The draws below stay inside these ranges and needn't reach their ends.
Inputs may be any that keep to these rules, and one draw needn't show every extreme that they name: `beam_taps`: a parent row n reads child rows n + t and n + t + 1.
All inputs are finite; a program needn't handle non-finite values.
Results may differ from the reference program's by a relative error of at most 0.019.
Values may be sent and summed in bfloat16 or wider, within the bound.
No kernel may reach another device: no remote copies, remote signals or barrier semaphores. Data moves between devices by JAX's collectives and lax.ppermute only.
A program may use at most 64 MiB of HBM per device.

```python
import jax
import jax.numpy as jnp
from jax import lax

R = 16384
RB = 128
LEVELS = 4
P_S = 32
SUBS = 64
NB = 128


def touch_ends(result, rng, least, top_value):
    extent = result.shape
    index_at = [jax.random.randint(jax.random.fold_in(rng, axis), (), 0, extent[axis]) for axis in range(len(extent))]
    result = result.at[tuple(index_at)].set(least)
    longest = extent.index(max(extent))
    index_at[longest] = (index_at[longest] + 1) % extent[longest]
    return result.at[tuple(index_at)].set(top_value)


def steps_of(stream_key, shape, cuts, smallest, high):
    factor_of = 1.0
    for dim, shards_of in cuts:
        steps = jax.random.uniform(jax.random.fold_in(jax.random.fold_in(stream_key, 6), dim), (shards_of,), jnp.float32, smallest / len(cuts), high / len(cuts))
        factor_of = factor_of * jnp.repeat(jnp.exp(steps), shape[dim] // shards_of).reshape((-1,) + (1,) * (len(shape) - 1 - dim))
    return factor_of


def scatter_about(stream_key, extent, spread, reach, cuts=(), kind=jnp.bfloat16):
    drawn = spread * jax.random.normal(stream_key, extent, jnp.float32)
    if cuts:
        drawn = drawn * steps_of(stream_key, extent, cuts, -0.22, 0.18)
    return jnp.clip(drawn, -reach, reach).astype(kind)


def setup_inputs(seed: int = 0) -> dict:
    keys = jax.random.split(jax.random.key(seed), 7)
    echoes = scatter_about(keys[0], (SUBS, P_S, 2, R), 1.0, 6.0, ((0, 32), (1, 16)))
    matched_filter = scatter_about(keys[1], (2, R), 1.0, 6.0, (), jnp.float32)
    steering = scatter_about(keys[2], (2, NB, P_S), P_S ** -0.5, 1.0, ((1, 16),))
    kernels = scatter_about(keys[3], (LEVELS, 2, 2, RB, RB), (2 * RB) ** -0.5, 0.375)
    blend_gains = jnp.clip(jax.random.uniform(keys[4], (LEVELS, 2, 2, 2), jnp.float32, 0.3, 1.0), 0.3, 1.0)
    beam_taps = touch_ends(jax.random.randint(keys[5], (LEVELS, 2, 2, NB), -1, 1), jax.random.fold_in(keys[5], 1), -1, 0).astype(jnp.int32)
    return dict(echoes=echoes, matched_filter=matched_filter, steering=steering, kernels=kernels, blend_gains=blend_gains, beam_taps=beam_taps)


def merge_level(images, level, kernels, blend_gains, beam_taps):
    count = images.shape[0]
    rows = images.shape[1]
    low = 2 ** level
    high = count // (2 * low)
    padded = jnp.pad(images, ((0, 0), (1, 1), (0, 0), (0, 0)))
    split = padded.reshape((high, 2, low) + padded.shape[1:])
    results = []
    for parity in range(2):
        total = jnp.zeros((high, low, rows, 2, images.shape[-1]), jnp.float32)
        for child in range(2):
            source = split[:, child]
            shift = beam_taps[level, child, parity]
            index = jnp.arange(rows, dtype=jnp.int32) + shift.astype(jnp.int32) + 1
            first = jnp.take(source, index, axis=2).astype(jnp.float32)
            second = jnp.take(source, index + 1, axis=2).astype(jnp.float32)
            blend = (blend_gains[level, child, parity, 0] * first + blend_gains[level, child, parity, 1] * second).astype(jnp.bfloat16)
            real_in = blend[:, :, :, 0, :].astype(jnp.float32)
            imag_in = blend[:, :, :, 1, :].astype(jnp.float32)
            real_w = kernels[level, child, 0].astype(jnp.float32)
            imag_w = kernels[level, child, 1].astype(jnp.float32)
            out_real = jnp.einsum("ablk,kj->ablj", real_in, real_w) - jnp.einsum("ablk,kj->ablj", imag_in, imag_w)
            out_imag = jnp.einsum("ablk,kj->ablj", real_in, imag_w) + jnp.einsum("ablk,kj->ablj", imag_in, real_w)
            total = total + jnp.stack([out_real, out_imag], axis=3)
        results.append(total.astype(jnp.bfloat16))
    merged = jnp.stack(results, axis=1)
    return merged.reshape(images.shape)


def reference(echoes, matched_filter, steering, kernels, blend_gains, beam_taps):
    signal = lax.complex(echoes[:, :, 0].astype(jnp.float32), echoes[:, :, 1].astype(jnp.float32))
    matched = lax.complex(matched_filter[0], matched_filter[1])
    back = jnp.fft.ifft(jnp.fft.fft(signal, axis=-1) * matched, axis=-1)
    compressed = jnp.stack([jnp.real(back), jnp.imag(back)], axis=2).astype(jnp.bfloat16)
    blocks = compressed.reshape(SUBS, P_S, 2, R // RB, RB)
    blocks = jnp.moveaxis(blocks, 3, 0)
    steer = steering.astype(jnp.float32)
    mixing = jnp.stack([jnp.stack([steer[0], -steer[1]]), jnp.stack([steer[1], steer[0]])])

    def one_block(piece):
        images = jnp.einsum("oinp,spir->snor", mixing, piece.astype(jnp.float32)).astype(jnp.bfloat16)
        for level in range(LEVELS):
            images = merge_level(images, level, kernels, blend_gains, beam_taps)
        return images

    merged = lax.map(one_block, blocks)
    return jnp.moveaxis(merged, 0, 3).reshape(SUBS, NB, 2, R)
```

```python
import math

import jax
import jax.numpy as jnp
import numpy as np
from jax import lax
from jax.sharding import Mesh
from jax.sharding import PartitionSpec as P

FA = 128
LEVELS = 4
HIGH = lax.Precision.HIGH


def table_product(form, left, right):
    return jnp.einsum(form, left, right, precision=HIGH)


def dft_tables(order, sign, modulus):
    index = np.arange(order)
    phase = (index[:, None] * index[None, :]) % modulus
    angle = phase * (sign * 2.0 * math.pi / modulus)
    return (jnp.asarray(np.cos(angle), jnp.float32), jnp.asarray(np.sin(angle), jnp.float32))


def four_step(real_part, imag_part, sign):
    order = real_part.shape[-1]
    cos_small, sin_small = dft_tables(order, sign, order)
    cos_turn, sin_turn = dft_tables(order, sign, order * order)
    first_real = table_product("kn,qnm->qkm", cos_small, real_part) - table_product(
        "kn,qnm->qkm", sin_small, imag_part
    )
    first_imag = table_product("kn,qnm->qkm", cos_small, imag_part) + table_product(
        "kn,qnm->qkm", sin_small, real_part
    )
    turned_real = first_real * cos_turn - first_imag * sin_turn
    turned_imag = first_real * sin_turn + first_imag * cos_turn
    out_real = table_product("qkm,mj->qjk", turned_real, cos_small) - table_product(
        "qkm,mj->qjk", turned_imag, sin_small
    )
    out_imag = table_product("qkm,mj->qjk", turned_real, sin_small) + table_product(
        "qkm,mj->qjk", turned_imag, cos_small
    )
    return (out_real, out_imag)


def compress(echoes, matched_filter):
    count = echoes.shape[0] * echoes.shape[1]
    length = echoes.shape[-1]
    signal = echoes.astype(jnp.float32).reshape(count, 2, FA, FA)
    spec_real, spec_imag = four_step(signal[:, 0], signal[:, 1], -1.0)
    matched = matched_filter.reshape(2, FA, FA)
    prod_real = spec_real * matched[0] - spec_imag * matched[1]
    prod_imag = spec_real * matched[1] + spec_imag * matched[0]
    back_real, back_imag = four_step(prod_real, prod_imag, 1.0)
    stacked = jnp.stack([back_real, back_imag], axis=1) / length
    return stacked.reshape(echoes.shape[:3] + (FA, FA)).astype(jnp.bfloat16)


def as_blocks(pair):
    real_part, imag_part = pair[..., 0, :, :], pair[..., 1, :, :]
    top = jnp.concatenate([real_part, imag_part], axis=-1)
    bottom = jnp.concatenate([-imag_part, real_part], axis=-1)
    return jnp.concatenate([top, bottom], axis=-2)


def pick(table, index):
    return lax.dynamic_index_in_dim(table, index, 0, keepdims=False)


def range_chain(kernels, bits):
    blocks = as_blocks(kernels.astype(jnp.float32))
    chain = pick(blocks[3], bits[2])
    chain = table_product("ik,kj->ij", pick(blocks[2], bits[1]), chain)
    chain = table_product("ik,kj->ij", pick(blocks[1], bits[0]), chain)
    return table_product("cik,kj->cij", blocks[0], chain).astype(jnp.bfloat16)


def band_matrices(taps, gains):
    rows = taps.shape[0]
    first = jnp.moveaxis(taps, 0, -1).astype(jnp.int32)[..., None] + jnp.arange(rows)[:, None]
    column = jnp.arange(rows)
    lower = jnp.where(column == first, gains[..., 0, None, None], 0.0)
    upper = jnp.where(column == first + 1, gains[..., 1, None, None], 0.0)
    return lower + upper


def local(echoes, matched_filter, steering, kernels, blend_gains, beam_taps):
    zh = lax.axis_index("zh")
    zl = lax.axis_index("zl")
    own_rows = steering.shape[1]
    pulses = steering.shape[2]
    own_pulses = echoes.shape[1]
    beams = pulses // own_pulses

    packed = jnp.concatenate(
        [
            jnp.moveaxis(steering, 1, 0).reshape(own_rows, 2 * pulses),
            jnp.moveaxis(beam_taps, 3, 0).reshape(own_rows, 4 * LEVELS).astype(jnp.bfloat16),
        ],
        axis=1,
    )
    packed = jnp.pad(packed, ((0, 0), (0, 128 - packed.shape[1])))
    packed = lax.all_gather(packed, "beam", axis=0, tiled=True)
    rows = packed.shape[0]

    compressed = compress(echoes, matched_filter)
    mats = range_chain(kernels, (zl & 1, zl >> 1, zh)).reshape(2, 2, FA, 2, FA)
    turned = jnp.einsum(
        "spinm,simoj->sponj", compressed, mats, preferred_element_type=jnp.float32
    ).astype(jnp.bfloat16)
    width = 2 * own_pulses * 2
    peers = 4 * beams
    message = jnp.moveaxis(turned.reshape(width, peers, -1), 1, 0)
    own = lax.all_to_all(message, ("zl", "beam"), 0, 0, tiled=True).reshape(peers * width, -1)
    other = lax.ppermute(own, "zh", [(0, 1), (1, 0)])

    steer = packed[:, : 2 * pulses].astype(jnp.float32).reshape(rows, 2, beams, own_pulses)
    taps = packed[:, 2 * pulses : 2 * pulses + 4 * LEVELS].reshape(rows, LEVELS, 2, 2)
    band = band_matrices(taps, blend_gains)
    mixing = jnp.stack(
        [jnp.stack([steer[:, 0], -steer[:, 1]], -1), jnp.stack([steer[:, 1], steer[:, 0]], -1)], 1
    )
    lead = table_product("cenm,mobpi->enobcpi", band[0], mixing).reshape(2, rows, -1)
    lead = table_product("cenm,fmx->cefnx", band[1], lead)
    lead = table_product("cenm,dfgmx->cdefgnx", band[2], lead)

    def last(child):
        b4 = pick(pick(band[3], child), zh)
        full = table_product("nm,cdefgmx->cdefgnx", b4, lead).astype(jnp.bfloat16)
        full = full.reshape(2, 2, 2, 2, 2, beams, own_rows, 2, FA)
        full = jnp.transpose(full, (2, 3, 5, 4, 7, 6, 0, 1, 8))
        return full.reshape(4 * beams * 2 * 2 * own_rows, 4 * FA)

    total = jnp.dot(last(zh), own, preferred_element_type=jnp.float32)
    total = total + jnp.dot(last(1 - zh), other, preferred_element_type=jnp.float32)
    result = total.astype(jnp.bfloat16).reshape(peers, 2 * 2 * own_rows, -1)
    arrived = lax.all_to_all(result, ("zl", "beam"), 0, 0, tiled=True)
    arrived = arrived.reshape(peers, 2, 2, own_rows, -1)
    return jnp.transpose(arrived, (1, 3, 2, 0, 4)).reshape(2, own_rows, 2, -1)


def solution(mesh):
    fine = Mesh(mesh.devices.reshape(4, 2, 4, 16), ("g", "zh", "zl", "beam"))
    sub = ("g", "zh", "zl")
    return jax.shard_map(
        local,
        mesh=fine,
        in_specs=(
            P(sub, "beam", None, None),
            P(),
            P(None, "beam", None),
            P(),
            P(),
            P(None, None, None, "beam"),
        ),
        out_specs=P(sub, "beam", None, None),
        check_vma=False,
    )
```

```python
import math

import jax
import jax.numpy as jnp
import ml_dtypes
import numpy as np
from jax import lax
from jax.experimental import pallas as pl
from jax.experimental.pallas import tpu as pltpu
from jax.sharding import Mesh
from jax.sharding import PartitionSpec as P

FA = 128
LEVELS = 4
BF16 = jnp.bfloat16
F32 = jnp.float32


def halves(table):
    high = table.astype(ml_dtypes.bfloat16)
    low = (table - high.astype(np.float64)).astype(ml_dtypes.bfloat16)
    return np.stack([high, low])


def dft_blocks():
    index = np.arange(FA)
    product = index[:, None] * index[None, :]
    angle = (product % FA) * (2.0 * math.pi / FA)
    c, s = np.cos(angle), np.sin(angle)
    turn = (product % (FA * FA)) * (2.0 * math.pi / (FA * FA))
    return (
        halves(np.block([[c, s], [-s, c]])),
        halves(np.block([[c, -s], [s, c]])),
        np.stack([np.cos(turn), np.sin(turn)]).astype(np.float32),
    )


def split(value):
    high = value.astype(BF16)
    return high, (value - high.astype(F32)).astype(BF16)


def dot(left, right):
    return jnp.dot(left, right, preferred_element_type=F32)


def dot_table(value, table):
    high, low = split(value)
    return dot(high, table[0]) + dot(low, table[0]) + dot(high, table[1])


def table_dot(table, value):
    high, low = split(value)
    return dot(table[0], high) + dot(table[0], low) + dot(table[1], high)


def complex_block(ref, *index):
    real_part, imag_part = ref[(*index, 0)], ref[(*index, 1)]
    top = jnp.concatenate([real_part, imag_part], axis=1)
    return jnp.concatenate([top, jnp.concatenate([-imag_part, real_part], axis=1)], axis=0)


def compress_kernel(bits, echo, matched, kern, packed, plus, minus, turn, out, rows):
    count = echo.shape[0]
    width = 2 * count
    c, s = turn[0], turn[1]

    chain = complex_block(kern, 3, bits[2]).astype(F32)
    for level in (2, 1):
        high, low = split(chain)
        block = complex_block(kern, level, bits[level - 1])
        chain = dot(block, high) + dot(block, low)
    high, low = split(chain)
    mats = []
    for child in range(2):
        block = complex_block(kern, 0, child)
        mats.append((dot(block, high) + dot(block, low)).astype(BF16))

    signal = jnp.concatenate([echo[q].reshape(2 * FA, FA) for q in range(count)], axis=1)
    first = dot(plus[0], signal) + dot(plus[1], signal)
    stacked = []
    for q in range(count):
        real_part = first[:FA, q * FA : (q + 1) * FA]
        imag_part = first[FA:, q * FA : (q + 1) * FA]
        stacked.append(
            jnp.concatenate([real_part * c + imag_part * s, imag_part * c - real_part * s], axis=1)
        )
    spectrum = dot_table(jnp.concatenate(stacked, axis=0), minus)

    scale = 1.0 / (FA * FA)
    filter_real = jnp.transpose(matched[0]) * scale
    filter_imag = jnp.transpose(matched[1]) * scale
    stacked = []
    for q in range(count):
        real_part = spectrum[q * FA : (q + 1) * FA, :FA]
        imag_part = spectrum[q * FA : (q + 1) * FA, FA:]
        stacked.append(
            jnp.concatenate(
                [
                    real_part * filter_real - imag_part * filter_imag,
                    real_part * filter_imag + imag_part * filter_real,
                ],
                axis=1,
            )
        )
    back = dot_table(jnp.concatenate(stacked, axis=0), plus)

    stacked = []
    for q in range(count):
        real_part = back[q * FA : (q + 1) * FA, :FA]
        imag_part = back[q * FA : (q + 1) * FA, FA:]
        stacked.append(
            jnp.concatenate([real_part * c - imag_part * s, imag_part * c + real_part * s], axis=0)
        )
    pulses = table_dot(minus, jnp.concatenate(stacked, axis=1)).astype(BF16)

    for q in range(count):
        lanes = slice(q * FA, (q + 1) * FA)
        pair = jnp.concatenate([pulses[:FA, lanes], pulses[FA:, lanes]], axis=1)
        turned = dot(pair, mats[q * 2 // count])
        rows[pl.ds(2 * q, FA, stride=width), :] = turned[:, :FA]
        rows[pl.ds(2 * q + 1, FA, stride=width), :] = turned[:, FA:]
    half = FA // 2
    for part in range(2):
        piece = rows[pl.ds(part * half * width, half * width), :]
        out[:, :, part * FA : (part + 1) * FA] = piece.reshape(half, width, FA).astype(BF16)
    out[:, :, 2 * FA :] = jnp.broadcast_to(packed[...][None], (half, width, FA))


def compress(bits, echo, matched, kern, packed):
    plus, minus, turn = dft_blocks()
    width = 2 * echo.shape[0]
    vmem = pl.BlockSpec(memory_space=pltpu.VMEM)
    return pl.pallas_call(
        compress_kernel,
        out_shape=jax.ShapeDtypeStruct((FA // 2, width, 3 * FA), BF16),
        in_specs=[pl.BlockSpec(memory_space=pltpu.SMEM)] + [vmem] * 7,
        out_specs=vmem,
        scratch_shapes=[pltpu.VMEM((FA * width, FA), F32)],
        compiler_params=pltpu.CompilerParams(vmem_limit_bytes=32 * 2**20),
        cost_estimate=pl.CostEstimate(flops=10**9, bytes_accessed=2 * 10**6, transcendentals=0),
    )(bits, echo, matched, kern, packed, jnp.asarray(plus), jnp.asarray(minus), jnp.asarray(turn))


def beam_kernel(steer_lanes, bits, gains, packed, mixing, out_own, out_other):
    e3 = pl.program_id(0) // 2
    e2 = pl.program_id(0) % 2
    e4 = bits[2]
    rows = packed.shape[0]
    data = packed[...]
    taps = data.astype(F32)
    row = lax.broadcasted_iota(jnp.int32, (rows, FA), 0)
    lane = lax.broadcasted_iota(jnp.int32, (rows, FA), 1)

    def weights(level, child, parity):
        at = steer_lanes + (level * 2 + child) * 2
        even, odd = taps[:, at : at + 1], taps[:, at + 1 : at + 2]
        if isinstance(parity, int):
            tap = odd if parity else even
        else:
            tap = jnp.where(parity == 1, odd, even)
        tap = jnp.broadcast_to(tap, (rows, FA))
        index = ((level * 2 + child) * 2 + parity) * 2
        g0, g1 = gains[index], gains[index + 1]
        backward = tap < 0
        before = jnp.where(backward & (row > 0), g0, 0.0)
        here = jnp.where(backward, g1, g0)
        after = jnp.where(jnp.logical_not(backward) & (row < rows - 1), g1, 0.0)
        return before, here, after

    def neighbours(value):
        return pltpu.roll(value, 1, 0), value, pltpu.roll(value, rows - 1, 0)

    def blend(near, weight):
        return near[0] * weight[0] + near[1] * weight[1] + near[2] * weight[2]

    second_child = (lane // 4) % 2 == 1
    levels = [[weights(level, child, parity) for child in range(2)] for level, parity in ((1, e2), (2, e3), (3, e4))]
    for e1 in range(2):
        pair = [weights(0, child, e1) for child in range(2)]
        lead = [jnp.where(second_child, odd, even) for even, odd in zip(*pair)]
        start = [blend(neighbours(dot(data, mixing[o])), lead) for o in range(2)]
        for c2 in range(2):
            mid = [blend(neighbours(v), levels[0][c2]) for v in start]
            for c3 in range(2):
                high = [neighbours(blend(neighbours(v), levels[1][c3])) for v in mid]
                lanes = slice((c3 * 2 + c2) * FA, (c3 * 2 + c2 + 1) * FA)
                for own, out in ((True, out_own), (False, out_other)):
                    weight = [
                        jnp.where((e4 == 0) == own, zero, one) for zero, one in zip(levels[2][0], levels[2][1])
                    ]
                    done = [blend(near, weight).reshape(rows // 8, 8, FA) for near in high]
                    out[0, :, e1, :, lanes] = jnp.concatenate(done, axis=1).astype(BF16)


def beam_factors(bits, gains, packed, beams, own_pulses):
    rows = packed.shape[0]
    pulses = beams * own_pulses
    mixing = np.zeros((2, FA, FA), ml_dtypes.bfloat16)
    for b in range(beams):
        for c1 in range(2):
            for p in range(own_pulses):
                for i in range(2):
                    lane = ((b * 2 + c1) * own_pulses + p) * 2 + i
                    pulse = b * own_pulses + p
                    mixing[0, i * pulses + pulse, lane] = -1 if i else 1
                    mixing[1, (1 - i) * pulses + pulse, lane] = 1
    shape = jax.ShapeDtypeStruct((4, rows // 8, 2, 16, 4 * FA), BF16)
    spec = pl.BlockSpec((1, rows // 8, 2, 16, 4 * FA), lambda g: (g, 0, 0, 0, 0))
    smem = pl.BlockSpec(memory_space=pltpu.SMEM)
    vmem = pl.BlockSpec(memory_space=pltpu.VMEM)

    def kernel(*refs):
        beam_kernel(2 * pulses, *refs)

    return pl.pallas_call(
        kernel,
        grid=(4,),
        out_shape=(shape, shape),
        in_specs=[smem, smem, vmem, vmem],
        out_specs=(spec, spec),
        compiler_params=pltpu.CompilerParams(vmem_limit_bytes=32 * 2**20),
        cost_estimate=pl.CostEstimate(flops=2 * 10**9, bytes_accessed=4 * 10**6, transcendentals=0),
    )(bits, gains, packed, jnp.asarray(mixing))


def local(echoes, matched_filter, steering, kernels, blend_gains, beam_taps):
    zh = lax.axis_index("zh")
    zl = lax.axis_index("zl")
    own_rows = steering.shape[1]
    pulses = steering.shape[2]
    own_pulses = echoes.shape[1]
    beams = pulses // own_pulses
    peers = 4 * beams
    bits = jnp.stack([zl & 1, zl >> 1, zh]).astype(jnp.int32)

    packed = jnp.concatenate(
        [
            jnp.moveaxis(steering, 1, 0).reshape(own_rows, 2 * pulses),
            jnp.moveaxis(beam_taps, 3, 0).reshape(own_rows, 4 * LEVELS).astype(BF16),
        ],
        axis=1,
    )
    packed = jnp.pad(packed, ((0, 0), (0, FA - packed.shape[1])))
    message = compress(
        bits, echoes.reshape(2 * own_pulses, 2, FA, FA), matched_filter.reshape(2, FA, FA), kernels, packed
    )
    arrived = lax.all_to_all(message, ("zl", "beam"), 0, 0, tiled=True)
    own = arrived[:, :, : 2 * FA].reshape(-1, 2 * FA)
    other = lax.ppermute(own, "zh", [(0, 1), (1, 0)])
    packed = arrived[:beams, :, 2 * FA :].reshape(-1, FA)
    near, far = beam_factors(bits, blend_gains.reshape(-1), packed, beams, own_pulses)

    total = dot(near.reshape(-1, 4 * FA), own)
    total = total + dot(far.reshape(-1, 4 * FA), other)
    result = total.astype(BF16).reshape(peers, 4 * own_rows, 2 * FA)
    arrived = lax.all_to_all(result, ("zl", "beam"), 0, 0, tiled=True)
    arrived = arrived.reshape(peers, 2, 2, own_rows, 2, FA)
    return jnp.transpose(arrived, (1, 3, 2, 4, 0, 5)).reshape(2, own_rows, 2, -1)


def solution(mesh):
    fine = Mesh(mesh.devices.reshape(4, 2, 4, 16), ("g", "zh", "zl", "beam"))
    sub = ("g", "zh", "zl")
    return jax.shard_map(
        local,
        mesh=fine,
        in_specs=(
            P(sub, "beam", None, None),
            P(),
            P(None, "beam", None),
            P(),
            P(),
            P(None, None, None, "beam"),
        ),
        out_specs=P(sub, "beam", None, None),
        check_vma=False,
    )
```

```python
import math

import jax
import jax.numpy as jnp
import ml_dtypes
import numpy as np
from jax import lax
from jax.experimental import pallas as pl
from jax.experimental.pallas import tpu as pltpu
from jax.sharding import Mesh
from jax.sharding import PartitionSpec as P

FA = 128
LEVELS = 4
BF16 = jnp.bfloat16
F32 = jnp.float32


def halves(table):
    high = table.astype(ml_dtypes.bfloat16)
    low = (table - high.astype(np.float64)).astype(ml_dtypes.bfloat16)
    return np.stack([high, low])


def dft_blocks():
    index = np.arange(FA)
    product = index[:, None] * index[None, :]
    angle = (product % FA) * (2.0 * math.pi / FA)
    c, s = np.cos(angle), np.sin(angle)
    turn = (product % (FA * FA)) * (2.0 * math.pi / (FA * FA))
    return (
        halves(np.block([[c, s], [-s, c]])),
        halves(np.block([[c, -s], [s, c]])),
        np.stack([np.cos(turn), np.sin(turn)]).astype(np.float32),
    )


def split(value):
    high = value.astype(BF16)
    return high, (value - high.astype(F32)).astype(BF16)


def dot(left, right):
    return jnp.dot(left, right, preferred_element_type=F32)


def dot_table(value, table):
    high, low = split(value)
    return dot(high, table[0]) + dot(low, table[0]) + dot(high, table[1])


def table_dot(table, value):
    high, low = split(value)
    return dot(table[0], high) + dot(table[0], low) + dot(table[1], high)


def complex_block(ref, *index):
    real_part, imag_part = ref[(*index, 0)], ref[(*index, 1)]
    top = jnp.concatenate([real_part, imag_part], axis=1)
    return jnp.concatenate([top, jnp.concatenate([-imag_part, real_part], axis=1)], axis=0)


def compress_kernel(children, carried, bits, echo, *refs):
    if carried:
        packed, refs = refs[0], refs[1:]
    matched_hbm, kern_hbm, plus_hbm, minus_hbm, turn_hbm, out = refs[:6]
    matched, kern, plus, minus, turn, rows, filters, sems = refs[6:]
    loads = [
        pltpu.make_async_copy(source, target, sems.at[at])
        for at, (source, target) in enumerate(
            ((kern_hbm, kern), (plus_hbm, plus), (turn_hbm, turn), (minus_hbm, minus), (matched_hbm, matched))
        )
    ]
    for load in loads:
        load.start()
    count = echo.shape[0]
    width = 2 * count

    loads[0].wait()
    chain = complex_block(kern, 3, bits[2]).astype(F32)
    for level in (2, 1):
        high, low = split(chain)
        block = complex_block(kern, level, bits[level - 1])
        chain = dot(block, high) + dot(block, low)
    high, low = split(chain)
    mats = []
    for child in range(children):
        block = complex_block(kern, 0, child)
        mats.append((dot(block, high) + dot(block, low)).astype(BF16))

    loads[1].wait()
    loads[2].wait()
    c, s = turn[0], turn[1]
    signal = jnp.concatenate([echo[q].reshape(2 * FA, FA) for q in range(count)], axis=1)
    first = dot(plus[0], signal) + dot(plus[1], signal)
    stacked = []
    for q in range(count):
        real_part = first[:FA, q * FA : (q + 1) * FA]
        imag_part = first[FA:, q * FA : (q + 1) * FA]
        stacked.append(
            jnp.concatenate([real_part * c + imag_part * s, imag_part * c - real_part * s], axis=1)
        )
    loads[3].wait()
    spectrum = dot_table(jnp.concatenate(stacked, axis=0), minus)

    loads[4].wait()
    for j in range(FA):
        filters[0, j : j + 1, :] = matched[0:1, j * FA : (j + 1) * FA]
        filters[1, j : j + 1, :] = matched[1:2, j * FA : (j + 1) * FA]
    scale = 1.0 / (FA * FA)
    filter_real = jnp.transpose(filters[0]) * scale
    filter_imag = jnp.transpose(filters[1]) * scale
    stacked = []
    for q in range(count):
        real_part = spectrum[q * FA : (q + 1) * FA, :FA]
        imag_part = spectrum[q * FA : (q + 1) * FA, FA:]
        stacked.append(
            jnp.concatenate(
                [
                    real_part * filter_real - imag_part * filter_imag,
                    real_part * filter_imag + imag_part * filter_real,
                ],
                axis=1,
            )
        )
    back = dot_table(jnp.concatenate(stacked, axis=0), plus)

    stacked = []
    for q in range(count):
        real_part = back[q * FA : (q + 1) * FA, :FA]
        imag_part = back[q * FA : (q + 1) * FA, FA:]
        stacked.append(
            jnp.concatenate([real_part * c - imag_part * s, imag_part * c + real_part * s], axis=0)
        )
    pulses = table_dot(minus, jnp.concatenate(stacked, axis=1)).astype(BF16)

    for q in range(count):
        lanes = slice(q * FA, (q + 1) * FA)
        pair = jnp.concatenate([pulses[:FA, lanes], pulses[FA:, lanes]], axis=1)
        turned = dot(pair, mats[q * children // count])
        rows[pl.ds(2 * q, FA, stride=width), :] = turned[:, :FA]
        rows[pl.ds(2 * q + 1, FA, stride=width), :] = turned[:, FA:]
    half = FA // 2
    for part in range(2):
        piece = rows[pl.ds(part * half * width, half * width), :]
        lanes = slice(part * FA, (part + 1) * FA)
        if carried:
            out[:, :, lanes] = piece.reshape(half, width, FA).astype(BF16)
        else:
            out[:, lanes] = piece.astype(BF16)
    if carried:
        out[:, :, 2 * FA :] = jnp.broadcast_to(packed[...][None], (half, width, FA))


def compress(bits, echo, matched, kern, packed=None):
    plus, minus, turn = (jnp.asarray(table) for table in dft_blocks())
    count = echo.shape[0]
    width = 2 * count
    carried = packed is not None
    vmem = pl.BlockSpec(memory_space=pltpu.VMEM)
    shape = (FA // 2, width, 3 * FA) if carried else (FA // 2 * width, 2 * FA)
    large = [matched, kern, plus, minus, turn]

    def kernel(*refs):
        compress_kernel(count // 2, carried, *refs)

    return pl.pallas_call(
        kernel,
        out_shape=jax.ShapeDtypeStruct(shape, BF16),
        in_specs=[pl.BlockSpec(memory_space=pltpu.SMEM)]
        + [vmem] * (1 + carried)
        + [pl.BlockSpec(memory_space=pl.ANY)] * len(large),
        out_specs=vmem,
        scratch_shapes=[pltpu.VMEM(table.shape, table.dtype) for table in large]
        + [
            pltpu.VMEM((FA * width, FA), F32),
            pltpu.VMEM((2, FA, FA), F32),
            pltpu.SemaphoreType.DMA((len(large),)),
        ],
        compiler_params=pltpu.CompilerParams(vmem_limit_bytes=60 * 2**20),
        cost_estimate=pl.CostEstimate(
            flops=10**9 if carried else 5 * 10**10, bytes_accessed=2 * 10**6, transcendentals=0
        ),
    )(bits, echo, *([packed] if carried else []), *large)


def beam_kernel(steer_lanes, bits, gains, packed, mixing, out_own, out_other):
    e3 = pl.program_id(0) // 2
    e2 = pl.program_id(0) % 2
    e4 = bits[2]
    rows = packed.shape[0]
    data = packed[...]
    taps = data.astype(F32)
    row = lax.broadcasted_iota(jnp.int32, (rows, FA), 0)
    lane = lax.broadcasted_iota(jnp.int32, (rows, FA), 1)

    def weights(level, child, parity):
        at = steer_lanes + (level * 2 + child) * 2
        even, odd = taps[:, at : at + 1], taps[:, at + 1 : at + 2]
        if isinstance(parity, int):
            tap = odd if parity else even
        else:
            tap = jnp.where(parity == 1, odd, even)
        tap = jnp.broadcast_to(tap, (rows, FA))
        index = ((level * 2 + child) * 2 + parity) * 2
        g0, g1 = gains[index], gains[index + 1]
        backward = tap < 0
        before = jnp.where(backward & (row > 0), g0, 0.0)
        here = jnp.where(backward, g1, g0)
        after = jnp.where(jnp.logical_not(backward) & (row < rows - 1), g1, 0.0)
        return before, here, after

    def neighbours(value):
        return pltpu.roll(value, 1, 0), value, pltpu.roll(value, rows - 1, 0)

    def blend(near, weight):
        return near[0] * weight[0] + near[1] * weight[1] + near[2] * weight[2]

    second_child = (lane // 4) % 2 == 1
    levels = [[weights(level, child, parity) for child in range(2)] for level, parity in ((1, e2), (2, e3), (3, e4))]
    for e1 in range(2):
        pair = [weights(0, child, e1) for child in range(2)]
        lead = [jnp.where(second_child, odd, even) for even, odd in zip(*pair)]
        start = [blend(neighbours(dot(data, mixing[o])), lead) for o in range(2)]
        for c2 in range(2):
            mid = [blend(neighbours(v), levels[0][c2]) for v in start]
            for c3 in range(2):
                high = [neighbours(blend(neighbours(v), levels[1][c3])) for v in mid]
                lanes = slice((c3 * 2 + c2) * FA, (c3 * 2 + c2 + 1) * FA)
                for own, out in ((True, out_own), (False, out_other)):
                    weight = [
                        jnp.where((e4 == 0) == own, zero, one) for zero, one in zip(levels[2][0], levels[2][1])
                    ]
                    done = [blend(near, weight).reshape(rows // 8, 8, FA) for near in high]
                    out[0, :, e1, :, lanes] = jnp.concatenate(done, axis=1).astype(BF16)


def beam_factors(bits, gains, packed, beams, own_pulses):
    rows = packed.shape[0]
    pulses = beams * own_pulses
    mixing = np.zeros((2, FA, FA), ml_dtypes.bfloat16)
    for b in range(beams):
        for c1 in range(2):
            for p in range(own_pulses):
                for i in range(2):
                    lane = ((b * 2 + c1) * own_pulses + p) * 2 + i
                    pulse = b * own_pulses + p
                    mixing[0, i * pulses + pulse, lane] = -1 if i else 1
                    mixing[1, (1 - i) * pulses + pulse, lane] = 1
    shape = jax.ShapeDtypeStruct((4, rows // 8, 2, 16, 4 * FA), BF16)
    spec = pl.BlockSpec((1, rows // 8, 2, 16, 4 * FA), lambda g: (g, 0, 0, 0, 0))
    smem = pl.BlockSpec(memory_space=pltpu.SMEM)
    vmem = pl.BlockSpec(memory_space=pltpu.VMEM)

    def kernel(*refs):
        beam_kernel(2 * pulses, *refs)

    return pl.pallas_call(
        kernel,
        grid=(4,),
        out_shape=(shape, shape),
        in_specs=[smem, smem, vmem, vmem],
        out_specs=(spec, spec),
        compiler_params=pltpu.CompilerParams(vmem_limit_bytes=32 * 2**20),
        cost_estimate=pl.CostEstimate(flops=2 * 10**9, bytes_accessed=4 * 10**6, transcendentals=0),
    )(bits, gains, packed, jnp.asarray(mixing))


def local(echoes, matched_filter, steering, kernels, blend_gains, beam_taps):
    zh = lax.axis_index("zh")
    zl = lax.axis_index("zl")
    own_rows = steering.shape[1]
    pulses = steering.shape[2]
    own_pulses = echoes.shape[1]
    beams = pulses // own_pulses
    peers = 4 * beams
    bits = jnp.stack([zl & 1, zl >> 1, zh]).astype(jnp.int32)
    far_bits = jnp.stack([zl & 1, zl >> 1, 1 - zh]).astype(jnp.int32)

    packed = jnp.concatenate(
        [
            jnp.moveaxis(steering, 1, 0).reshape(own_rows, 2 * pulses),
            jnp.moveaxis(beam_taps, 3, 0).reshape(own_rows, 4 * LEVELS).astype(BF16),
        ],
        axis=1,
    )
    packed = jnp.pad(packed, ((0, 0), (0, FA - packed.shape[1])))
    across = [(0, 1), (1, 0)]
    far_echoes = lax.ppermute(echoes[:1], "zh", across)
    message = compress(
        bits, echoes.reshape(2 * own_pulses, 2, FA, FA), matched_filter, kernels, packed
    )
    arrived = lax.all_to_all(message, ("zl", "beam"), 0, 0, tiled=True)
    own = arrived[:, :, : 2 * FA]
    width = own.shape[1]
    far_second = lax.ppermute(own[:, width // 2 :].reshape(-1, 2 * FA), "zh", across)
    far_message = compress(
        far_bits, far_echoes.reshape(own_pulses, 2, FA, FA), matched_filter, kernels
    )
    far_first = lax.all_to_all(
        far_message.reshape(peers, width // 2, 2 * FA), ("zl", "beam"), 0, 0, tiled=True
    )
    own = own.reshape(-1, 2 * FA)
    other = jnp.concatenate(
        [far_first, far_second.reshape(peers, width // 2, 2 * FA)], axis=1
    ).reshape(-1, 2 * FA)
    packed = arrived[:beams, :, 2 * FA :].reshape(-1, FA)
    near, far = beam_factors(bits, blend_gains.reshape(-1), packed, beams, own_pulses)

    total = dot(near.reshape(-1, 4 * FA), own)
    total = total + dot(far.reshape(-1, 4 * FA), other)
    result = total.astype(BF16).reshape(peers, 4 * own_rows, 2 * FA)
    arrived = lax.all_to_all(result, ("zl", "beam"), 0, 0, tiled=True)
    arrived = arrived.reshape(peers, 2, 2, own_rows, 2, FA)
    return jnp.transpose(arrived, (1, 3, 2, 4, 0, 5)).reshape(2, own_rows, 2, -1)


def solution(mesh):
    fine = Mesh(mesh.devices.reshape(4, 2, 4, 16), ("g", "zh", "zl", "beam"))
    sub = ("g", "zh", "zl")
    return jax.shard_map(
        local,
        mesh=fine,
        in_specs=(
            P(sub, "beam", None, None),
            P(),
            P(None, "beam", None),
            P(),
            P(),
            P(None, None, None, "beam"),
        ),
        out_specs=P(sub, "beam", None, None),
        check_vma=False,
    )
```

```python
import math

import jax
import jax.numpy as jnp
import ml_dtypes
import numpy as np
from jax import lax
from jax.experimental import pallas as pl
from jax.experimental.pallas import tpu as pltpu
from jax.sharding import Mesh
from jax.sharding import PartitionSpec as P

FA = 128
LEVELS = 4
BF16 = jnp.bfloat16
F32 = jnp.float32


def halves(table):
    high = table.astype(ml_dtypes.bfloat16)
    low = (table - high.astype(np.float64)).astype(ml_dtypes.bfloat16)
    return np.stack([high, low])


def dft_blocks():
    index = np.arange(FA)
    product = index[:, None] * index[None, :]
    angle = (product % FA) * (2.0 * math.pi / FA)
    c, s = np.cos(angle), np.sin(angle)
    turn = (product % (FA * FA)) * (2.0 * math.pi / (FA * FA))
    return (
        halves(np.block([[c, s], [-s, c]])),
        halves(np.block([[c, -s], [s, c]])),
        np.stack([np.cos(turn), np.sin(turn)]).astype(np.float32),
    )


def split(value):
    high = value.astype(BF16)
    return high, (value - high.astype(F32)).astype(BF16)


def dot(left, right):
    return jnp.dot(left, right, preferred_element_type=F32)


def dot_table(value, table):
    high, low = split(value)
    return dot(high, table[0]) + dot(low, table[0]) + dot(high, table[1])


def table_dot(table, value):
    high, low = split(value)
    return dot(table[0], high) + dot(table[0], low) + dot(table[1], high)


def complex_block(ref, *index):
    real_part, imag_part = ref[(*index, 0)], ref[(*index, 1)]
    top = jnp.concatenate([real_part, imag_part], axis=1)
    return jnp.concatenate([top, jnp.concatenate([-imag_part, real_part], axis=1)], axis=0)


def compress_kernel(children, bits, echo, *refs):
    matched_hbm, kern_hbm, plus_hbm, minus_hbm, turn_hbm, out = refs[:6]
    matched, kern, plus, minus, turn, rows, filters, sems = refs[6:]
    loads = [
        pltpu.make_async_copy(source, target, sems.at[at])
        for at, (source, target) in enumerate(
            ((kern_hbm, kern), (plus_hbm, plus), (turn_hbm, turn), (minus_hbm, minus), (matched_hbm, matched))
        )
    ]
    for load in loads:
        load.start()
    count = echo.shape[0]
    width = 2 * count

    loads[0].wait()
    chain = complex_block(kern, 3, bits[2]).astype(F32)
    for level in (2, 1):
        high, low = split(chain)
        block = complex_block(kern, level, bits[level - 1])
        chain = dot(block, high) + dot(block, low)
    high, low = split(chain)
    mats = []
    for child in range(children):
        block = complex_block(kern, 0, child)
        mats.append((dot(block, high) + dot(block, low)).astype(BF16))

    loads[1].wait()
    loads[2].wait()
    c, s = turn[0], turn[1]
    signal = jnp.concatenate([echo[q].reshape(2 * FA, FA) for q in range(count)], axis=1)
    first = dot(plus[0], signal) + dot(plus[1], signal)
    stacked = []
    for q in range(count):
        real_part = first[:FA, q * FA : (q + 1) * FA]
        imag_part = first[FA:, q * FA : (q + 1) * FA]
        stacked.append(
            jnp.concatenate([real_part * c + imag_part * s, imag_part * c - real_part * s], axis=1)
        )
    loads[3].wait()
    spectrum = dot_table(jnp.concatenate(stacked, axis=0), minus)

    loads[4].wait()
    for j in range(FA):
        filters[0, j : j + 1, :] = matched[0:1, j * FA : (j + 1) * FA]
        filters[1, j : j + 1, :] = matched[1:2, j * FA : (j + 1) * FA]
    scale = 1.0 / (FA * FA)
    filter_real = jnp.transpose(filters[0]) * scale
    filter_imag = jnp.transpose(filters[1]) * scale
    stacked = []
    for q in range(count):
        real_part = spectrum[q * FA : (q + 1) * FA, :FA]
        imag_part = spectrum[q * FA : (q + 1) * FA, FA:]
        stacked.append(
            jnp.concatenate(
                [
                    real_part * filter_real - imag_part * filter_imag,
                    real_part * filter_imag + imag_part * filter_real,
                ],
                axis=1,
            )
        )
    back = dot_table(jnp.concatenate(stacked, axis=0), plus)

    stacked = []
    for q in range(count):
        real_part = back[q * FA : (q + 1) * FA, :FA]
        imag_part = back[q * FA : (q + 1) * FA, FA:]
        stacked.append(
            jnp.concatenate([real_part * c - imag_part * s, imag_part * c + real_part * s], axis=0)
        )
    pulses = table_dot(minus, jnp.concatenate(stacked, axis=1)).astype(BF16)

    for q in range(count):
        lanes = slice(q * FA, (q + 1) * FA)
        pair = jnp.concatenate([pulses[:FA, lanes], pulses[FA:, lanes]], axis=1)
        turned = dot(pair, mats[q * children // count])
        rows[pl.ds(2 * q, FA, stride=width), :] = turned[:, :FA]
        rows[pl.ds(2 * q + 1, FA, stride=width), :] = turned[:, FA:]
    copies, slices = out.shape[:2]
    for part in range(FA // slices):
        piece = rows[pl.ds(part * slices * width, slices * width), :]
        piece = piece.reshape(slices, width, FA).astype(BF16)
        for copy in range(copies):
            out[copy, :, :, part * FA : (part + 1) * FA] = piece


def compress(bits, echo, matched, kern, copies, slices):
    plus, minus, turn = (jnp.asarray(table) for table in dft_blocks())
    count = echo.shape[0]
    width = 2 * count
    vmem = pl.BlockSpec(memory_space=pltpu.VMEM)
    large = [matched, kern, plus, minus, turn]

    def kernel(*refs):
        compress_kernel(2, *refs)

    return pl.pallas_call(
        kernel,
        out_shape=jax.ShapeDtypeStruct((copies, slices, width, FA * FA // slices), BF16),
        in_specs=[pl.BlockSpec(memory_space=pltpu.SMEM), vmem]
        + [pl.BlockSpec(memory_space=pl.ANY)] * len(large),
        out_specs=vmem,
        scratch_shapes=[pltpu.VMEM(table.shape, table.dtype) for table in large]
        + [
            pltpu.VMEM((FA * width, FA), F32),
            pltpu.VMEM((2, FA, FA), F32),
            pltpu.SemaphoreType.DMA((len(large),)),
        ],
        compiler_params=pltpu.CompilerParams(vmem_limit_bytes=60 * 2**20),
        cost_estimate=pl.CostEstimate(flops=5 * 10**10, bytes_accessed=2 * 10**6, transcendentals=0),
    )(bits, echo, *large)


def beam_kernel(steer_lanes, bits, gains, packed, mixing, out_own, out_other):
    e3 = pl.program_id(0) // 2
    e2 = pl.program_id(0) % 2
    e4, core = bits[2], bits[3]
    rows = packed.shape[0]
    data = packed[...]
    taps = data.astype(F32)
    row = lax.broadcasted_iota(jnp.int32, (rows, FA), 0)
    lane = lax.broadcasted_iota(jnp.int32, (rows, FA), 1)

    def weights(level, child, parity):
        at = steer_lanes + (level * 2 + child) * 2
        even, odd = taps[:, at : at + 1], taps[:, at + 1 : at + 2]
        if isinstance(parity, int):
            tap = odd if parity else even
        else:
            tap = jnp.where(parity == 1, odd, even)
        tap = jnp.broadcast_to(tap, (rows, FA))
        index = ((level * 2 + child) * 2 + parity) * 2
        g0, g1 = gains[index], gains[index + 1]
        backward = tap < 0
        before = jnp.where(backward & (row > 0), g0, 0.0)
        here = jnp.where(backward, g1, g0)
        after = jnp.where(jnp.logical_not(backward) & (row < rows - 1), g1, 0.0)
        return before, here, after

    def by_lane(level, parity, second):
        pair = [weights(level, child, parity) for child in range(2)]
        return [jnp.where(second, odd, even) for even, odd in zip(*pair)]

    def neighbours(value):
        return pltpu.roll(value, 1, 0), value, pltpu.roll(value, rows - 1, 0)

    def blend(near, weight):
        return near[0] * weight[0] + near[1] * weight[1] + near[2] * weight[2]

    def of_core(value):
        tiles = value.reshape(rows // 16, 2, 8, FA)
        return jnp.where(core == 0, tiles[:, 0], tiles[:, 1]).reshape(rows // 2, FA)

    level2 = by_lane(1, e2, lane >= FA // 2)
    level3 = [weights(2, child, e3) for child in range(2)]
    level4 = [[of_core(w) for w in weights(3, child, e4)] for child in range(2)]
    imaginary = lane[: rows // 2] % 2 == 1
    for e1 in range(2):
        level1 = by_lane(0, e1, (lane // 4) % 2 == 1)
        for slot, out in ((0, out_own), (1, out_other)):
            source = jnp.where(slot == 0, core, 1 - core)
            steer = dot(data, mixing[source])
            second = blend(neighbours(blend(neighbours(steer), level1)), level2)
            second = neighbours(second)
            for c3 in range(2):
                third = [of_core(v) for v in neighbours(blend(second, level3[c3]))]
                for c4 in range(2):
                    real_row = blend(third, level4[c4])
                    imag_row = jnp.where(
                        imaginary, pltpu.roll(real_row, 1, 1), -pltpu.roll(real_row, FA - 1, 1)
                    )
                    both = [v.reshape(rows // 16, 8, FA) for v in (real_row, imag_row)]
                    at = (c4 * 2 + c3) * FA
                    out[0, :, e1, :, at : at + FA] = jnp.concatenate(both, axis=1).astype(BF16)


def beam_factors(bits, gains, packed, beams, own_pulses):
    rows = packed.shape[0]
    pulses = beams * own_pulses
    chips = beams // 2
    mixing = np.zeros((2, FA, FA), ml_dtypes.bfloat16)
    for core, c2, chip, c1, p, i in np.ndindex(2, 2, chips, 2, own_pulses, 2):
        lane = (((c2 * chips + chip) * 2 + c1) * own_pulses + p) * 2 + i
        mixing[core, i * pulses + (chip * 2 + core) * own_pulses + p, lane] = -1 if i else 1
    shape = jax.ShapeDtypeStruct((4, chips, 2, 16, 4 * FA), BF16)
    spec = pl.BlockSpec((1, chips, 2, 16, 4 * FA), lambda g: (g, 0, 0, 0, 0))
    smem = pl.BlockSpec(memory_space=pltpu.SMEM)
    vmem = pl.BlockSpec(memory_space=pltpu.VMEM)

    def kernel(*refs):
        beam_kernel(2 * pulses, *refs)

    return pl.pallas_call(
        kernel,
        grid=(4,),
        out_shape=(shape, shape),
        in_specs=[smem, smem, vmem, vmem],
        out_specs=(spec, spec),
        compiler_params=pltpu.CompilerParams(vmem_limit_bytes=32 * 2**20),
        cost_estimate=pl.CostEstimate(flops=2 * 10**9, bytes_accessed=4 * 10**6, transcendentals=0),
    )(bits, gains, packed, jnp.asarray(mixing))


def local(echoes, matched_filter, steering, kernels, blend_gains, beam_taps):
    zh = lax.axis_index("zh")
    zl = lax.axis_index("zl")
    own_rows = steering.shape[1]
    pulses = steering.shape[2]
    own_pulses = echoes.shape[1]
    beams = pulses // own_pulses
    slices = 4 * beams // 2
    bits = jnp.stack([zl & 1, zl >> 1, zh, lax.axis_index("core")]).astype(jnp.int32)

    packed = jnp.concatenate(
        [
            jnp.moveaxis(steering, 1, 0).reshape(own_rows, 2 * pulses),
            jnp.moveaxis(beam_taps, 3, 0).reshape(own_rows, 4 * LEVELS).astype(BF16),
        ],
        axis=1,
    )
    packed = jnp.pad(packed, ((0, 0), (0, FA - packed.shape[1])))
    packed = jnp.broadcast_to(packed, (beams,) + packed.shape)
    packed = lax.all_to_all(packed, ("chip", "core"), 0, 0, tiled=True).reshape(-1, FA)
    message = compress(
        bits, echoes.reshape(2 * own_pulses, 2, FA, FA), matched_filter, kernels, 2, slices
    )
    width = message.shape[2]
    message, packed = lax.optimization_barrier((message, packed))
    own = lax.all_to_all(
        message.reshape(2 * slices, width, -1), ("zh", "zl", "chip"), 0, 0, tiled=True
    ).reshape(2 * slices * width, -1)
    near, far = beam_factors(bits, blend_gains.reshape(-1), packed, beams, own_pulses)
    other = lax.ppermute(own, "core", [(0, 1), (1, 0)])

    total = dot(near.reshape(-1, 4 * FA), own)
    total = total + dot(far.reshape(-1, 4 * FA), other)
    result = total.astype(BF16).reshape(slices, 4 * own_rows, -1)
    arrived = lax.all_to_all(result, ("zl", "chip"), 0, 0, tiled=True)
    arrived = arrived.reshape(slices, 2, 2, own_rows, -1, FA)
    return jnp.transpose(arrived, (1, 3, 2, 4, 0, 5)).reshape(2, own_rows, 2, -1)


def solution(mesh):
    fine = Mesh(mesh.devices.reshape(4, 2, 4, 8, 2), ("g", "zh", "zl", "chip", "core"))
    sub = ("g", "zh", "zl")
    beam = ("chip", "core")
    return jax.shard_map(
        local,
        mesh=fine,
        in_specs=(
            P(sub, beam, None, None),
            P(),
            P(None, beam, None),
            P(),
            P(),
            P(None, None, None, beam),
        ),
        out_specs=P(sub, beam, None, None),
        check_vma=False,
    )
```

```python
import math

import jax
import jax.numpy as jnp
import ml_dtypes
import numpy as np
from jax import lax
from jax.experimental import pallas as pl
from jax.experimental.pallas import tpu as pltpu
from jax.sharding import Mesh
from jax.sharding import PartitionSpec as P

FA = 128
LEVELS = 4
BF16 = jnp.bfloat16
F32 = jnp.float32


def halves(table):
    high = table.astype(ml_dtypes.bfloat16)
    low = (table - high.astype(np.float64)).astype(ml_dtypes.bfloat16)
    return np.stack([high, low])


def dft_blocks():
    index = np.arange(FA)
    product = index[:, None] * index[None, :]
    angle = (product % FA) * (2.0 * math.pi / FA)
    c, s = np.cos(angle), np.sin(angle)
    turn = (product % (FA * FA)) * (2.0 * math.pi / (FA * FA))
    return (
        halves(np.block([[c, s], [-s, c]])),
        halves(np.block([[c, -s], [s, c]])),
        np.stack([np.cos(turn), np.sin(turn)]).astype(np.float32),
    )


def split(value):
    high = value.astype(BF16)
    return high, (value - high.astype(F32)).astype(BF16)


def dot(left, right):
    return jnp.dot(left, right, preferred_element_type=F32)


def dot_table(value, table):
    high, low = split(value)
    return dot(high, table[0]) + dot(low, table[0]) + dot(high, table[1])


def table_dot(table, value):
    high, low = split(value)
    return dot(table[0], high) + dot(table[0], low) + dot(table[1], high)


def complex_block(ref, *index):
    real_part, imag_part = ref[(*index, 0)], ref[(*index, 1)]
    top = jnp.concatenate([real_part, imag_part], axis=1)
    return jnp.concatenate([top, jnp.concatenate([-imag_part, real_part], axis=1)], axis=0)


def range_matrices(bits, kern):
    chain = complex_block(kern, 3, bits[2]).astype(F32)
    for level in (2, 1):
        high, low = split(chain)
        block = complex_block(kern, level, bits[level - 1])
        chain = dot(block, high) + dot(block, low)
    high, low = split(chain)
    mats = []
    for child in range(2):
        block = complex_block(kern, 0, child)
        mats.append((dot(block, high) + dot(block, low)).astype(BF16))
    return mats


def forward_left(echo, plus, turn):
    count = echo.shape[0]
    c, s = turn[0], turn[1]
    signal = jnp.concatenate([echo[q].reshape(2 * FA, FA) for q in range(count)], axis=1)
    first = dot(plus[0], signal) + dot(plus[1], signal)
    stacked = []
    for q in range(count):
        real_part = first[:FA, q * FA : (q + 1) * FA]
        imag_part = first[FA:, q * FA : (q + 1) * FA]
        stacked.append(
            jnp.concatenate([real_part * c + imag_part * s, imag_part * c - real_part * s], axis=1)
        )
    return jnp.concatenate(stacked, axis=0)


def filtered(spectrum, filters):
    stacked = []
    for q in range(spectrum.shape[0] // FA):
        real_part = spectrum[q * FA : (q + 1) * FA, :FA]
        imag_part = spectrum[q * FA : (q + 1) * FA, FA:]
        stacked.append(
            jnp.concatenate(
                [
                    real_part * filters[0] - imag_part * filters[1],
                    real_part * filters[1] + imag_part * filters[0],
                ],
                axis=1,
            )
        )
    return jnp.concatenate(stacked, axis=0)


def inverse_left(back, minus, turn):
    c, s = turn[0], turn[1]
    stacked = []
    for q in range(back.shape[0] // FA):
        real_part = back[q * FA : (q + 1) * FA, :FA]
        imag_part = back[q * FA : (q + 1) * FA, FA:]
        stacked.append(
            jnp.concatenate([real_part * c - imag_part * s, imag_part * c + real_part * s], axis=0)
        )
    return table_dot(minus, jnp.concatenate(stacked, axis=1)).astype(BF16)


def times_range(pulses, mats, rows):
    count = pulses.shape[1] // FA
    for q in range(count):
        lanes = slice(q * FA, (q + 1) * FA)
        pair = jnp.concatenate([pulses[:FA, lanes], pulses[FA:, lanes]], axis=1)
        turned = dot(pair, mats[q * 2 // count])
        rows[pl.ds(2 * q, FA, stride=2 * count), :] = turned[:, :FA]
        rows[pl.ds(2 * q + 1, FA, stride=2 * count), :] = turned[:, FA:]


def own_kernel(bits, echo, matched_hbm, kern_hbm, plus_hbm, minus_hbm, turn_hbm, rows, filters, *refs):
    matched, kern, plus, minus, turn, lines, sems = refs
    loads = [
        pltpu.make_async_copy(source, target, sems.at[at])
        for at, (source, target) in enumerate(
            ((kern_hbm, kern), (plus_hbm, plus), (turn_hbm, turn), (minus_hbm, minus), (matched_hbm, matched))
        )
    ]
    for load in loads:
        load.start()
    loads[0].wait()
    mats = range_matrices(bits, kern)
    loads[1].wait()
    loads[2].wait()
    turned = forward_left(echo, plus, turn)
    loads[3].wait()
    spectrum = dot_table(turned, minus)
    loads[4].wait()
    for j in range(FA):
        lines[0, j : j + 1, :] = matched[0:1, j * FA : (j + 1) * FA]
        lines[1, j : j + 1, :] = matched[1:2, j * FA : (j + 1) * FA]
    scale = 1.0 / (FA * FA)
    filters[0] = jnp.transpose(lines[0]) * scale
    filters[1] = jnp.transpose(lines[1]) * scale
    back = dot_table(filtered(spectrum, filters), plus)
    times_range(inverse_left(back, minus, turn), mats, rows)


def far_kernel(bits, echo, near_rows, filters, kern, plus, minus, turn, out, rows):
    mats = range_matrices(bits, kern)
    spectrum = dot_table(forward_left(echo, plus, turn), minus)
    back = dot_table(filtered(spectrum, filters), plus)
    times_range(inverse_left(back, minus, turn), mats, rows)
    slices = out.shape[0]
    width = rows.shape[0] // FA
    for part in range(FA // slices):
        at = pl.ds(part * slices * width, slices * width)
        pieces = [v[at, :].reshape(slices, width, FA) for v in (near_rows, rows)]
        out[:, :, part * FA : (part + 1) * FA] = jnp.concatenate(pieces, axis=1).astype(BF16)


SMEM = pl.BlockSpec(memory_space=pltpu.SMEM)
VMEM = pl.BlockSpec(memory_space=pltpu.VMEM)
ANY = pl.BlockSpec(memory_space=pl.ANY)


def compress_own(bits, echo, matched, kern, tables):
    large = [matched, kern, *tables]
    return pl.pallas_call(
        own_kernel,
        out_shape=(
            jax.ShapeDtypeStruct((FA * 2 * echo.shape[0], FA), F32),
            jax.ShapeDtypeStruct((2, FA, FA), F32),
        ),
        in_specs=[SMEM, VMEM] + [ANY] * len(large),
        out_specs=(VMEM, VMEM),
        scratch_shapes=[pltpu.VMEM(table.shape, table.dtype) for table in large]
        + [pltpu.VMEM((2, FA, FA), F32), pltpu.SemaphoreType.DMA((len(large),))],
        compiler_params=pltpu.CompilerParams(vmem_limit_bytes=32 * 2**20),
        cost_estimate=pl.CostEstimate(flops=10**9, bytes_accessed=2 * 10**6, transcendentals=0),
    )(bits, echo, *large)


def compress_far(bits, echo, near_rows, filters, kern, tables, slices):
    width = 2 * echo.shape[0]
    return pl.pallas_call(
        far_kernel,
        out_shape=jax.ShapeDtypeStruct((slices, 2 * width, FA * FA // slices), BF16),
        in_specs=[SMEM] + [VMEM] * (4 + len(tables)),
        out_specs=VMEM,
        scratch_shapes=[pltpu.VMEM((FA * width, FA), F32)],
        compiler_params=pltpu.CompilerParams(vmem_limit_bytes=32 * 2**20),
        cost_estimate=pl.CostEstimate(flops=10**9, bytes_accessed=2 * 10**6, transcendentals=0),
    )(bits, echo, near_rows, filters, kern, *tables)


def beam_kernel(steer_lanes, bits, gains, packed, mixing, out_own, out_other):
    e3 = pl.program_id(0) // 2
    e2 = pl.program_id(0) % 2
    e4, core = bits[2], bits[3]
    rows = packed.shape[0]
    data = packed[...]
    taps = data.astype(F32)
    row = lax.broadcasted_iota(jnp.int32, (rows, FA), 0)
    lane = lax.broadcasted_iota(jnp.int32, (rows, FA), 1)

    def weights(level, child, parity):
        at = steer_lanes + (level * 2 + child) * 2
        even, odd = taps[:, at : at + 1], taps[:, at + 1 : at + 2]
        if isinstance(parity, int):
            tap = odd if parity else even
        else:
            tap = jnp.where(parity == 1, odd, even)
        tap = jnp.broadcast_to(tap, (rows, FA))
        index = ((level * 2 + child) * 2 + parity) * 2
        g0, g1 = gains[index], gains[index + 1]
        backward = tap < 0
        before = jnp.where(backward & (row > 0), g0, 0.0)
        here = jnp.where(backward, g1, g0)
        after = jnp.where(jnp.logical_not(backward) & (row < rows - 1), g1, 0.0)
        return before, here, after

    def by_lane(level, parity, second):
        pair = [weights(level, child, parity) for child in range(2)]
        return [jnp.where(second, odd, even) for even, odd in zip(*pair)]

    def neighbours(value):
        return pltpu.roll(value, 1, 0), value, pltpu.roll(value, rows - 1, 0)

    def blend(near, weight):
        return near[0] * weight[0] + near[1] * weight[1] + near[2] * weight[2]

    def of_core(value):
        tiles = value.reshape(rows // 16, 2, 8, FA)
        return jnp.where(core == 0, tiles[:, 0], tiles[:, 1]).reshape(rows // 2, FA)

    level2 = [weights(1, child, e2) for child in range(2)]
    level3 = [weights(2, child, e3) for child in range(2)]
    near_child, far_child = ([jnp.where(e4 == at, *v) for v in zip(weights(3, 0, e4), weights(3, 1, e4))] for at in (0, 1))
    level4 = [of_core(jnp.where((lane // 8) % 2 == 0, *v)) for v in zip(near_child, far_child)]
    imaginary = lane[: rows // 2] % 2 == 1
    for e1 in range(2):
        level1 = by_lane(0, e1, (lane // 4) % 2 == 1)
        for slot, out in ((0, out_own), (1, out_other)):
            source = jnp.where(slot == 0, core, 1 - core)
            first = neighbours(blend(neighbours(dot(data, mixing[source])), level1))
            for c2 in range(2):
                second = neighbours(blend(first, level2[c2]))
                for c3 in range(2):
                    third = [of_core(v) for v in neighbours(blend(second, level3[c3]))]
                    real_row = blend(third, level4)
                    imag_row = jnp.where(
                        imaginary, pltpu.roll(real_row, 1, 1), -pltpu.roll(real_row, FA - 1, 1)
                    )
                    both = [v.reshape(rows // 16, 8, FA) for v in (real_row, imag_row)]
                    at = (c3 * 2 + c2) * FA
                    out[0, :, e1, :, at : at + FA] = jnp.concatenate(both, axis=1).astype(BF16)


def beam_factors(bits, gains, packed, beams, own_pulses):
    rows = packed.shape[0]
    pulses = beams * own_pulses
    chips = beams // 2
    mixing = np.zeros((2, FA, FA), ml_dtypes.bfloat16)
    for core, chip, half, c1, p, i in np.ndindex(2, chips, 2, 2, own_pulses, 2):
        lane = (((chip * 2 + half) * 2 + c1) * own_pulses + p) * 2 + i
        mixing[core, i * pulses + (chip * 2 + core) * own_pulses + p, lane] = -1 if i else 1
    shape = jax.ShapeDtypeStruct((4, chips, 2, 16, 4 * FA), BF16)
    spec = pl.BlockSpec((1, chips, 2, 16, 4 * FA), lambda g: (g, 0, 0, 0, 0))
    def kernel(*refs):
        beam_kernel(2 * pulses, *refs)

    return pl.pallas_call(
        kernel,
        grid=(4,),
        out_shape=(shape, shape),
        in_specs=[SMEM, SMEM, VMEM, VMEM],
        out_specs=(spec, spec),
        compiler_params=pltpu.CompilerParams(vmem_limit_bytes=32 * 2**20),
        cost_estimate=pl.CostEstimate(flops=3 * 10**10, bytes_accessed=4 * 10**6, transcendentals=0),
    )(bits, gains, packed, jnp.asarray(mixing))


def local(echoes, matched_filter, steering, kernels, blend_gains, beam_taps):
    zh = lax.axis_index("zh")
    zl = lax.axis_index("zl")
    own_rows = steering.shape[1]
    pulses = steering.shape[2]
    own_pulses = echoes.shape[1]
    beams = pulses // own_pulses
    slices = 4 * beams // 2
    core = lax.axis_index("core")
    bits = jnp.stack([zl & 1, zl >> 1, zh, core]).astype(jnp.int32)
    far_bits = jnp.stack([zl & 1, zl >> 1, 1 - zh, core]).astype(jnp.int32)
    swap = [(0, 1), (1, 0)]
    tables = [jnp.asarray(table) for table in dft_blocks()]
    blocks = (2 * own_pulses, 2, FA, FA)

    far_echoes = lax.ppermute(echoes, "zh", swap)
    packed = jnp.concatenate(
        [
            jnp.moveaxis(steering, 1, 0).reshape(own_rows, 2 * pulses),
            jnp.moveaxis(beam_taps, 3, 0).reshape(own_rows, 4 * LEVELS).astype(BF16),
        ],
        axis=1,
    )
    packed = jnp.pad(packed, ((0, 0), (0, FA - packed.shape[1])))
    packed = jnp.broadcast_to(packed, (beams,) + packed.shape)
    packed = lax.all_to_all(packed, ("chip", "core"), 0, 0, tiled=True).reshape(-1, FA)
    rows, filters = compress_own(bits, echoes.reshape(blocks), matched_filter, kernels, tables)
    message = compress_far(far_bits, far_echoes.reshape(blocks), rows, filters, kernels, tables, slices)
    message, packed = lax.optimization_barrier((message, packed))
    own = lax.all_to_all(message, ("zl", "chip"), 0, 0, tiled=True)
    own = own.reshape(slices * message.shape[1], -1)
    near, far = beam_factors(bits, blend_gains.reshape(-1), packed, beams, own_pulses)
    own, near, far = lax.optimization_barrier((own, near, far))
    other = lax.ppermute(own, "core", swap)

    total = dot(near.reshape(-1, 4 * FA), own)
    total = total + dot(far.reshape(-1, 4 * FA), other)
    result = total.astype(BF16).reshape(slices, 4 * own_rows, -1)
    arrived = lax.all_to_all(result, ("zl", "chip"), 0, 0, tiled=True)
    arrived = arrived.reshape(slices, 2, 2, own_rows, -1, FA)
    return jnp.transpose(arrived, (1, 3, 2, 4, 0, 5)).reshape(2, own_rows, 2, -1)


def solution(mesh):
    fine = Mesh(mesh.devices.reshape(4, 2, 4, 8, 2), ("g", "zh", "zl", "chip", "core"))
    sub = ("g", "zh", "zl")
    beam = ("chip", "core")
    return jax.shard_map(
        local,
        mesh=fine,
        in_specs=(
            P(sub, beam, None, None),
            P(),
            P(None, beam, None),
            P(),
            P(),
            P(None, None, None, beam),
        ),
        out_specs=P(sub, beam, None, None),
        check_vma=False,
    )
```

```python
import math

import jax
import jax.numpy as jnp
import ml_dtypes
import numpy as np
from jax import lax
from jax.experimental import pallas as pl
from jax.experimental.pallas import tpu as pltpu
from jax.sharding import Mesh
from jax.sharding import PartitionSpec as P

FA = 128
LEVELS = 4
BF16 = jnp.bfloat16
F32 = jnp.float32


def halves(table):
    high = table.astype(ml_dtypes.bfloat16)
    low = (table - high.astype(np.float64)).astype(ml_dtypes.bfloat16)
    return np.stack([high, low])


def dft_blocks():
    index = np.arange(FA)
    product = index[:, None] * index[None, :]
    angle = (product % FA) * (2.0 * math.pi / FA)
    c, s = np.cos(angle), np.sin(angle)
    turn = (product % (FA * FA)) * (2.0 * math.pi / (FA * FA))
    return (
        halves(np.block([[c, s], [-s, c]])),
        halves(np.block([[c, -s], [s, c]])),
        np.stack([np.cos(turn), np.sin(turn)]).astype(np.float32),
    )


def split(value):
    high = value.astype(BF16)
    return high, (value - high.astype(F32)).astype(BF16)


def dot(left, right):
    return jnp.dot(left, right, preferred_element_type=F32)


def dot_table(value, table):
    high, low = split(value)
    return dot(high, table[0]) + dot(low, table[0]) + dot(high, table[1])


def table_dot(table, value):
    high, low = split(value)
    return dot(table[0], high) + dot(table[0], low) + dot(table[1], high)


def complex_block(ref, *index):
    real_part, imag_part = ref[(*index, 0)], ref[(*index, 1)]
    top = jnp.concatenate([real_part, imag_part], axis=1)
    return jnp.concatenate([top, jnp.concatenate([-imag_part, real_part], axis=1)], axis=0)


def range_matrices(bits, kern):
    chain = complex_block(kern, 3, bits[2]).astype(F32)
    for level in (2, 1):
        high, low = split(chain)
        block = complex_block(kern, level, bits[level - 1])
        chain = dot(block, high) + dot(block, low)
    high, low = split(chain)
    mats = []
    for child in range(2):
        block = complex_block(kern, 0, child)
        mats.append((dot(block, high) + dot(block, low)).astype(BF16))
    return mats


def forward_left(echo, plus, turn):
    count = echo.shape[0]
    c, s = turn[0], turn[1]
    signal = jnp.concatenate([echo[q].reshape(2 * FA, FA) for q in range(count)], axis=1)
    first = dot(plus[0], signal) + dot(plus[1], signal)
    stacked = []
    for q in range(count):
        real_part = first[:FA, q * FA : (q + 1) * FA]
        imag_part = first[FA:, q * FA : (q + 1) * FA]
        stacked.append(
            jnp.concatenate([real_part * c + imag_part * s, imag_part * c - real_part * s], axis=1)
        )
    return jnp.concatenate(stacked, axis=0)


def filtered(spectrum, filters):
    stacked = []
    for q in range(spectrum.shape[0] // FA):
        real_part = spectrum[q * FA : (q + 1) * FA, :FA]
        imag_part = spectrum[q * FA : (q + 1) * FA, FA:]
        stacked.append(
            jnp.concatenate(
                [
                    real_part * filters[0] - imag_part * filters[1],
                    real_part * filters[1] + imag_part * filters[0],
                ],
                axis=1,
            )
        )
    return jnp.concatenate(stacked, axis=0)


def inverse_left(back, minus, turn):
    c, s = turn[0], turn[1]
    stacked = []
    for q in range(back.shape[0] // FA):
        real_part = back[q * FA : (q + 1) * FA, :FA]
        imag_part = back[q * FA : (q + 1) * FA, FA:]
        stacked.append(
            jnp.concatenate([real_part * c - imag_part * s, imag_part * c + real_part * s], axis=0)
        )
    return table_dot(minus, jnp.concatenate(stacked, axis=1)).astype(BF16)


def times_range(pulses, mats, rows):
    count = pulses.shape[1] // FA
    for q in range(count):
        lanes = slice(q * FA, (q + 1) * FA)
        pair = jnp.concatenate([pulses[:FA, lanes], pulses[FA:, lanes]], axis=1)
        turned = dot(pair, mats[q * 2 // count])
        rows[pl.ds(2 * q, FA, stride=2 * count), :] = turned[:, :FA]
        rows[pl.ds(2 * q + 1, FA, stride=2 * count), :] = turned[:, FA:]


def send_order(rows, out):
    slices, width = out.shape[:2]
    for part in range(FA // slices):
        piece = rows[pl.ds(part * slices * width, slices * width), :]
        out[:, :, part * FA : (part + 1) * FA] = piece.reshape(slices, width, FA).astype(BF16)


def own_kernel(bits, echo, packed, matched_hbm, kern_hbm, plus_hbm, minus_hbm, turn_hbm, out, filters, *refs):
    matched, kern, plus, minus, turn, lines, rows, sems = refs
    loads = [
        pltpu.make_async_copy(source, target, sems.at[at])
        for at, (source, target) in enumerate(
            ((kern_hbm, kern), (plus_hbm, plus), (turn_hbm, turn), (minus_hbm, minus), (matched_hbm, matched))
        )
    ]
    for load in loads:
        load.start()
    loads[0].wait()
    mats = range_matrices(bits, kern)
    loads[1].wait()
    loads[2].wait()
    turned = forward_left(echo, plus, turn)
    loads[3].wait()
    spectrum = dot_table(turned, minus)
    loads[4].wait()
    for j in range(FA):
        lines[0, j : j + 1, :] = matched[0:1, j * FA : (j + 1) * FA]
        lines[1, j : j + 1, :] = matched[1:2, j * FA : (j + 1) * FA]
    scale = 1.0 / (FA * FA)
    filters[0] = jnp.transpose(lines[0]) * scale
    filters[1] = jnp.transpose(lines[1]) * scale
    back = dot_table(filtered(spectrum, filters), plus)
    times_range(inverse_left(back, minus, turn), mats, rows)
    send_order(rows, out)
    slices, width = out.shape[:2]
    out[:, :, out.shape[2] - FA :] = jnp.broadcast_to(packed[...][None], (slices, width, FA))


def far_kernel(bits, echo, filters, kern, plus, minus, turn, out, rows):
    mats = range_matrices(bits, kern)
    spectrum = dot_table(forward_left(echo, plus, turn), minus)
    back = dot_table(filtered(spectrum, filters), plus)
    times_range(inverse_left(back, minus, turn), mats, rows)
    send_order(rows, out)


SMEM = pl.BlockSpec(memory_space=pltpu.SMEM)
VMEM = pl.BlockSpec(memory_space=pltpu.VMEM)
ANY = pl.BlockSpec(memory_space=pl.ANY)


def compress_own(bits, echo, packed, matched, kern, tables, slices):
    large = [matched, kern, *tables]
    width = 2 * echo.shape[0]
    return pl.pallas_call(
        own_kernel,
        out_shape=(
            jax.ShapeDtypeStruct((slices, width, FA * FA // slices + FA), BF16),
            jax.ShapeDtypeStruct((2, FA, FA), F32),
        ),
        in_specs=[SMEM, VMEM, VMEM] + [ANY] * len(large),
        out_specs=(VMEM, VMEM),
        scratch_shapes=[pltpu.VMEM(table.shape, table.dtype) for table in large]
        + [
            pltpu.VMEM((2, FA, FA), F32),
            pltpu.VMEM((FA * width, FA), F32),
            pltpu.SemaphoreType.DMA((len(large),)),
        ],
        compiler_params=pltpu.CompilerParams(vmem_limit_bytes=60 * 2**20),
        cost_estimate=pl.CostEstimate(flops=10**9, bytes_accessed=2 * 10**6, transcendentals=0),
    )(bits, echo, packed, *large)


def compress_far(bits, echo, filters, kern, tables, slices):
    width = 2 * echo.shape[0]
    return pl.pallas_call(
        far_kernel,
        out_shape=jax.ShapeDtypeStruct((slices, width, FA * FA // slices), BF16),
        in_specs=[SMEM] + [VMEM] * (3 + len(tables)),
        out_specs=VMEM,
        scratch_shapes=[pltpu.VMEM((FA * width, FA), F32)],
        compiler_params=pltpu.CompilerParams(vmem_limit_bytes=32 * 2**20),
        cost_estimate=pl.CostEstimate(flops=6 * 10**10, bytes_accessed=2 * 10**6, transcendentals=0),
    )(bits, echo, filters, kern, *tables)


def beam_kernel(steer_lanes, bits, gains, packed, mixing, out_near, out_far):
    e3 = pl.program_id(0) // 2
    e2 = pl.program_id(0) % 2
    e4, core = bits[2], bits[3]
    rows = packed.shape[0]
    data = packed[...]
    taps = data.astype(F32)
    row = lax.broadcasted_iota(jnp.int32, (rows, FA), 0)
    lane = lax.broadcasted_iota(jnp.int32, (rows, FA), 1)

    def weights(level, child, parity):
        at = steer_lanes + (level * 2 + child) * 2
        even, odd = taps[:, at : at + 1], taps[:, at + 1 : at + 2]
        if isinstance(parity, int):
            tap = odd if parity else even
        else:
            tap = jnp.where(parity == 1, odd, even)
        tap = jnp.broadcast_to(tap, (rows, FA))
        index = ((level * 2 + child) * 2 + parity) * 2
        g0, g1 = gains[index], gains[index + 1]
        backward = tap < 0
        before = jnp.where(backward & (row > 0), g0, 0.0)
        here = jnp.where(backward, g1, g0)
        after = jnp.where(jnp.logical_not(backward) & (row < rows - 1), g1, 0.0)
        return before, here, after

    def by_lane(level, parity, second):
        pair = [weights(level, child, parity) for child in range(2)]
        return [jnp.where(second, odd, even) for even, odd in zip(*pair)]

    def neighbours(value):
        return pltpu.roll(value, 1, 0), value, pltpu.roll(value, rows - 1, 0)

    def blend(near, weight):
        return near[0] * weight[0] + near[1] * weight[1] + near[2] * weight[2]

    def of_core(value):
        tiles = value.reshape(rows // 16, 2, 8, FA)
        return jnp.where(core == 0, tiles[:, 0], tiles[:, 1]).reshape(rows // 2, FA)

    level2 = by_lane(1, e2, lane >= FA // 2)
    level3 = [weights(2, child, e3) for child in range(2)]
    pair = [weights(3, child, e4) for child in range(2)]
    level4 = [[of_core(jnp.where(e4 == at, *v)) for v in zip(pair[0], pair[1])] for at in (0, 1)]
    imaginary = lane[: rows // 2] % 2 == 1
    for e1 in range(2):
        level1 = by_lane(0, e1, (lane // 4) % 2 == 1)
        for slot in range(2):
            source = jnp.where(slot == 0, core, 1 - core)
            second = blend(neighbours(dot(data, mixing[source])), level1)
            second = neighbours(blend(neighbours(second), level2))
            for c3 in range(2):
                third = [of_core(v) for v in neighbours(blend(second, level3[c3]))]
                for half, out in ((0, out_near), (1, out_far)):
                    real_row = blend(third, level4[half])
                    imag_row = jnp.where(
                        imaginary, pltpu.roll(real_row, 1, 1), -pltpu.roll(real_row, FA - 1, 1)
                    )
                    both = [v.reshape(rows // 16, 8, FA) for v in (real_row, imag_row)]
                    at = (slot * 2 + c3) * FA
                    out[0, :, e1, :, at : at + FA] = jnp.concatenate(both, axis=1).astype(BF16)


def beam_factors(bits, gains, packed, beams, own_pulses):
    rows = packed.shape[0]
    pulses = beams * own_pulses
    chips = beams // 2
    mixing = np.zeros((2, FA, FA), ml_dtypes.bfloat16)
    for core, c2, chip, c1, p, i in np.ndindex(2, 2, chips, 2, own_pulses, 2):
        lane = (((c2 * chips + chip) * 2 + c1) * own_pulses + p) * 2 + i
        mixing[core, i * pulses + (chip * 2 + core) * own_pulses + p, lane] = -1 if i else 1
    shape = jax.ShapeDtypeStruct((4, chips, 2, 16, 4 * FA), BF16)
    spec = pl.BlockSpec((1, chips, 2, 16, 4 * FA), lambda g: (g, 0, 0, 0, 0))
    def kernel(*refs):
        beam_kernel(2 * pulses, *refs)

    return pl.pallas_call(
        kernel,
        grid=(4,),
        out_shape=(shape, shape),
        in_specs=[SMEM, SMEM, VMEM, VMEM],
        out_specs=(spec, spec),
        compiler_params=pltpu.CompilerParams(vmem_limit_bytes=32 * 2**20),
        cost_estimate=pl.CostEstimate(flops=3 * 10**10, bytes_accessed=4 * 10**6, transcendentals=0),
    )(bits, gains, packed, jnp.asarray(mixing))


def local(echoes, matched_filter, steering, kernels, blend_gains, beam_taps):
    zh = lax.axis_index("zh")
    zl = lax.axis_index("zl")
    own_rows = steering.shape[1]
    pulses = steering.shape[2]
    own_pulses = echoes.shape[1]
    beams = pulses // own_pulses
    slices = 4 * beams // 2
    core = lax.axis_index("core")
    bits = jnp.stack([zl & 1, zl >> 1, zh, core]).astype(jnp.int32)
    far_bits = jnp.stack([zl & 1, zl >> 1, 1 - zh, core]).astype(jnp.int32)
    swap = [(0, 1), (1, 0)]
    tables = [jnp.asarray(table) for table in dft_blocks()]
    blocks = (2 * own_pulses, 2, FA, FA)

    far_echoes = lax.ppermute(echoes, "zh", swap)
    packed = jnp.concatenate(
        [
            jnp.moveaxis(steering, 1, 0).reshape(own_rows, 2 * pulses),
            jnp.moveaxis(beam_taps, 3, 0).reshape(own_rows, 4 * LEVELS).astype(BF16),
        ],
        axis=1,
    )
    packed = jnp.pad(packed, ((0, 0), (0, FA - packed.shape[1])))
    message, filters = compress_own(
        bits, echoes.reshape(blocks), packed, matched_filter, kernels, tables, slices
    )
    far_message = compress_far(far_bits, far_echoes.reshape(blocks), filters, kernels, tables, slices)
    arrived = lax.all_to_all(message, ("zl", "chip"), 0, 0, tiled=True)
    far_message, arrived = lax.optimization_barrier((far_message, arrived))
    far_own = lax.all_to_all(far_message, ("zl", "chip"), 0, 0, tiled=True)

    arrived = arrived.reshape(-1, arrived.shape[2])
    swapped = lax.ppermute(arrived, "core", swap)
    split_at = arrived.shape[1] - FA
    chips = beams // 2
    packed = [v[: chips * own_rows, split_at:].reshape(chips, own_rows, FA) for v in (arrived, swapped)]
    packed = jnp.where(core == 0, jnp.stack(packed, axis=1), jnp.stack(packed[::-1], axis=1))
    near, far = beam_factors(
        bits, blend_gains.reshape(-1), packed.reshape(-1, FA), beams, own_pulses
    )
    near, far = (v.reshape(-1, 4 * FA) for v in (near, far))
    total = dot(near[:, : 2 * FA], arrived[:, :split_at]) + dot(near[:, 2 * FA :], swapped[:, :split_at])

    far_own, total, far = lax.optimization_barrier((far_own.reshape(-1, split_at), total, far))
    far_swapped = lax.ppermute(far_own, "core", swap)
    total = total + dot(far[:, : 2 * FA], far_own)
    total = total + dot(far[:, 2 * FA :], far_swapped)
    result = total.astype(BF16).reshape(slices, 4 * own_rows, -1)
    arrived = lax.all_to_all(result, ("zl", "chip"), 0, 0, tiled=True)
    arrived = arrived.reshape(slices, 2, 2, own_rows, -1, FA)
    return jnp.transpose(arrived, (1, 3, 2, 4, 0, 5)).reshape(2, own_rows, 2, -1)


def solution(mesh):
    fine = Mesh(mesh.devices.reshape(4, 2, 4, 8, 2), ("g", "zh", "zl", "chip", "core"))
    sub = ("g", "zh", "zl")
    beam = ("chip", "core")
    return jax.shard_map(
        local,
        mesh=fine,
        in_specs=(
            P(sub, beam, None, None),
            P(),
            P(None, beam, None),
            P(),
            P(),
            P(None, None, None, beam),
        ),
        out_specs=P(sub, beam, None, None),
        check_vma=False,
    )
```

```python
import math

import jax
import jax.numpy as jnp
import ml_dtypes
import numpy as np
from jax import lax
from jax.experimental import pallas as pl
from jax.experimental.pallas import tpu as pltpu
from jax.sharding import Mesh
from jax.sharding import PartitionSpec as P

FA = 128
LEVELS = 4
BF16 = jnp.bfloat16
F32 = jnp.float32


def halves(table):
    high = table.astype(ml_dtypes.bfloat16)
    low = (table - high.astype(np.float64)).astype(ml_dtypes.bfloat16)
    return np.stack([high, low])


def dft_blocks():
    index = np.arange(FA)
    product = index[:, None] * index[None, :]
    angle = (product % FA) * (2.0 * math.pi / FA)
    c, s = np.cos(angle), np.sin(angle)
    turn = (product % (FA * FA)) * (2.0 * math.pi / (FA * FA))
    return (
        halves(np.block([[c, s], [-s, c]])),
        halves(np.block([[c, -s], [s, c]])),
        np.stack([np.cos(turn), np.sin(turn)]).astype(np.float32),
    )


def split(value):
    high = value.astype(BF16)
    return high, (value - high.astype(F32)).astype(BF16)


def dot(left, right):
    return jnp.dot(left, right, preferred_element_type=F32)


def dot_table(value, table):
    high, low = split(value)
    return dot(high, table[0]) + dot(low, table[0]) + dot(high, table[1])


def table_dot(table, value):
    high, low = split(value)
    return dot(table[0], high) + dot(table[0], low) + dot(table[1], high)


def complex_block(ref, *index):
    real_part, imag_part = ref[(*index, 0)], ref[(*index, 1)]
    top = jnp.concatenate([real_part, imag_part], axis=1)
    return jnp.concatenate([top, jnp.concatenate([-imag_part, real_part], axis=1)], axis=0)


def place_bits(place):
    value = place[0]
    return (value >> 1) & 1, (value >> 2) & 1, (value >> 3) & 1, value & 1


def range_matrices(bits, kern):
    chain = complex_block(kern, 3, bits[2]).astype(F32)
    for level in (2, 1):
        high, low = split(chain)
        block = complex_block(kern, level, bits[level - 1])
        chain = dot(block, high) + dot(block, low)
    high, low = split(chain)
    mats = []
    for child in range(2):
        block = complex_block(kern, 0, child)
        mats.append((dot(block, high) + dot(block, low)).astype(BF16))
    return mats


def forward_left(echo, plus, turn):
    count = echo.shape[0]
    c, s = turn[0], turn[1]
    signal = jnp.concatenate([echo[q].reshape(2 * FA, FA) for q in range(count)], axis=1)
    first = dot(plus[0], signal) + dot(plus[1], signal)
    stacked = []
    for q in range(count):
        real_part = first[:FA, q * FA : (q + 1) * FA]
        imag_part = first[FA:, q * FA : (q + 1) * FA]
        stacked.append(
            jnp.concatenate([real_part * c + imag_part * s, imag_part * c - real_part * s], axis=1)
        )
    return jnp.concatenate(stacked, axis=0)


def filtered(spectrum, filters):
    stacked = []
    for q in range(spectrum.shape[0] // FA):
        real_part = spectrum[q * FA : (q + 1) * FA, :FA]
        imag_part = spectrum[q * FA : (q + 1) * FA, FA:]
        stacked.append(
            jnp.concatenate(
                [
                    real_part * filters[0] - imag_part * filters[1],
                    real_part * filters[1] + imag_part * filters[0],
                ],
                axis=1,
            )
        )
    return jnp.concatenate(stacked, axis=0)


def inverse_left(back, minus, turn):
    c, s = turn[0], turn[1]
    stacked = []
    for q in range(back.shape[0] // FA):
        real_part = back[q * FA : (q + 1) * FA, :FA]
        imag_part = back[q * FA : (q + 1) * FA, FA:]
        stacked.append(
            jnp.concatenate([real_part * c - imag_part * s, imag_part * c + real_part * s], axis=0)
        )
    return table_dot(minus, jnp.concatenate(stacked, axis=1)).astype(BF16)


def times_range(pulses, mats, rows):
    count = pulses.shape[1] // FA
    for q in range(count):
        lanes = slice(q * FA, (q + 1) * FA)
        pair = jnp.concatenate([pulses[:FA, lanes], pulses[FA:, lanes]], axis=1)
        turned = dot(pair, mats[q * 2 // count])
        rows[pl.ds(2 * q, FA, stride=2 * count), :] = turned[:, :FA]
        rows[pl.ds(2 * q + 1, FA, stride=2 * count), :] = turned[:, FA:]


def send_order(rows, out):
    slices, width = out.shape[:2]
    for part in range(FA // slices):
        piece = rows[pl.ds(part * slices * width, slices * width), :]
        out[:, :, part * FA : (part + 1) * FA] = piece.reshape(slices, width, FA).astype(BF16)


def own_kernel(
    place, steer, taps, echo_hbm, matched_hbm, kern_hbm, plus_hbm, minus_hbm, turn_hbm, out, filters, *refs
):
    echo, matched, kern, plus, minus, turn, lines, rows, packed, sems = refs
    loads = [
        pltpu.make_async_copy(source, target, sems.at[at])
        for at, (source, target) in enumerate(
            (
                (kern_hbm, kern),
                (plus_hbm, plus),
                (echo_hbm, echo),
                (turn_hbm, turn),
                (minus_hbm, minus),
                (matched_hbm, matched),
            )
        )
    ]
    for load in loads:
        load.start()
    packed[...] = jnp.zeros_like(packed)
    count, span = steer.shape[1], steer.shape[2]
    for i in range(2):
        packed[:, i * span : (i + 1) * span] = steer[i].astype(F32)
    for level, child, parity in np.ndindex(*taps.shape[:3]):
        row, lane = level * 2 + child, 2 * span + parity * count
        packed[row : row + 1, lane : lane + count] = taps[level, child, parity : parity + 1, :].astype(F32)
    loads[0].wait()
    mats = range_matrices(place_bits(place), kern)
    for load in loads[1:4]:
        load.wait()
    turned = forward_left(echo, plus, turn)
    loads[4].wait()
    spectrum = dot_table(turned, minus)
    loads[5].wait()
    for j in range(FA):
        lines[0, j : j + 1, :] = matched[0:1, j * FA : (j + 1) * FA]
        lines[1, j : j + 1, :] = matched[1:2, j * FA : (j + 1) * FA]
    scale = 1.0 / (FA * FA)
    filters[0] = jnp.transpose(lines[0]) * scale
    filters[1] = jnp.transpose(lines[1]) * scale
    back = dot_table(filtered(spectrum, filters), plus)
    times_range(inverse_left(back, minus, turn), mats, rows)
    send_order(rows, out)
    slices, width = out.shape[:2]
    out[:, :, out.shape[2] - FA :] = jnp.broadcast_to(packed[...].astype(BF16)[None], (slices, width, FA))


def far_kernel(place, echo, filters_hbm, kern, plus, minus, turn, out, rows, filters, sem):
    load = pltpu.make_async_copy(filters_hbm, filters, sem)
    load.start()
    low, middle, high, _ = place_bits(place)
    mats = range_matrices((low, middle, 1 - high), kern)
    spectrum = dot_table(forward_left(echo, plus, turn), minus)
    load.wait()
    back = dot_table(filtered(spectrum, filters), plus)
    times_range(inverse_left(back, minus, turn), mats, rows)
    send_order(rows, out)


SMEM = pl.BlockSpec(memory_space=pltpu.SMEM)
VMEM = pl.BlockSpec(memory_space=pltpu.VMEM)
ANY = pl.BlockSpec(memory_space=pl.ANY)


def compress_own(place, steering, taps, echo, matched, kern, tables, slices):
    large = [echo, matched, kern, *tables]
    width = 2 * echo.shape[0]
    return pl.pallas_call(
        own_kernel,
        out_shape=(
            jax.ShapeDtypeStruct((slices, width, FA * FA // slices + FA), BF16),
            jax.ShapeDtypeStruct((2, FA, FA), F32),
        ),
        in_specs=[SMEM, VMEM, VMEM] + [ANY] * len(large),
        out_specs=(VMEM, VMEM),
        scratch_shapes=[pltpu.VMEM(table.shape, table.dtype) for table in large]
        + [
            pltpu.VMEM((2, FA, FA), F32),
            pltpu.VMEM((FA * width, FA), F32),
            pltpu.VMEM((8, FA), F32),
            pltpu.SemaphoreType.DMA((len(large),)),
        ],
        compiler_params=pltpu.CompilerParams(vmem_limit_bytes=60 * 2**20),
        cost_estimate=pl.CostEstimate(flops=10**9, bytes_accessed=2 * 10**6, transcendentals=0),
    )(place, steering, taps, *large)


def compress_far(place, echo, filters, kern, tables, slices):
    width = 2 * echo.shape[0]
    return pl.pallas_call(
        far_kernel,
        out_shape=jax.ShapeDtypeStruct((slices, width, FA * FA // slices), BF16),
        in_specs=[SMEM, VMEM, ANY] + [VMEM] * (1 + len(tables)),
        out_specs=VMEM,
        scratch_shapes=[
            pltpu.VMEM((FA * width, FA), F32),
            pltpu.VMEM(filters.shape, F32),
            pltpu.SemaphoreType.DMA,
        ],
        compiler_params=pltpu.CompilerParams(vmem_limit_bytes=32 * 2**20),
        cost_estimate=pl.CostEstimate(flops=6 * 10**10, bytes_accessed=2 * 10**6, transcendentals=0),
    )(place, echo, filters, kern, *tables)


def beam_kernel(steer_lanes, place, gains, packed, mixing, out_near, out_far):
    e3 = pl.program_id(0) // 2
    e2 = pl.program_id(0) % 2
    _, _, e4, core = place_bits(place)
    rows = packed.shape[0]
    data = packed[...]
    taps = data.astype(F32)
    row = lax.broadcasted_iota(jnp.int32, (rows, FA), 0)
    lane = lax.broadcasted_iota(jnp.int32, (rows, FA), 1)

    def weights(level, child, parity):
        at = steer_lanes + (level * 2 + child) * 2
        even, odd = taps[:, at : at + 1], taps[:, at + 1 : at + 2]
        if isinstance(parity, int):
            tap = odd if parity else even
        else:
            tap = jnp.where(parity == 1, odd, even)
        tap = jnp.broadcast_to(tap, (rows, FA))
        index = ((level * 2 + child) * 2 + parity) * 2
        g0, g1 = gains[index], gains[index + 1]
        backward = tap < 0
        before = jnp.where(backward & (row > 0), g0, 0.0)
        here = jnp.where(backward, g1, g0)
        after = jnp.where(jnp.logical_not(backward) & (row < rows - 1), g1, 0.0)
        return before, here, after

    def by_lane(level, parity, second):
        pair = [weights(level, child, parity) for child in range(2)]
        return [jnp.where(second, odd, even) for even, odd in zip(*pair)]

    def neighbours(value):
        return pltpu.roll(value, 1, 0), value, pltpu.roll(value, rows - 1, 0)

    def blend(near, weight):
        return near[0] * weight[0] + near[1] * weight[1] + near[2] * weight[2]

    def of_core(value):
        tiles = value.reshape(rows // 16, 2, 8, FA)
        return jnp.where(core == 0, tiles[:, 0], tiles[:, 1]).reshape(rows // 2, FA)

    level2 = by_lane(1, e2, lane >= FA // 2)
    level3 = [weights(2, child, e3) for child in range(2)]
    pair = [weights(3, child, e4) for child in range(2)]
    level4 = [[of_core(jnp.where(e4 == at, *v)) for v in zip(pair[0], pair[1])] for at in (0, 1)]
    imaginary = lane[: rows // 2] % 2 == 1
    for e1 in range(2):
        level1 = by_lane(0, e1, (lane // 4) % 2 == 1)
        for slot in range(2):
            source = jnp.where(slot == 0, core, 1 - core)
            second = blend(neighbours(dot(data, mixing[source])), level1)
            second = neighbours(blend(neighbours(second), level2))
            for c3 in range(2):
                third = [of_core(v) for v in neighbours(blend(second, level3[c3]))]
                for half, out in ((0, out_near), (1, out_far)):
                    real_row = blend(third, level4[half])
                    imag_row = jnp.where(
                        imaginary, pltpu.roll(real_row, 1, 1), -pltpu.roll(real_row, FA - 1, 1)
                    )
                    both = [v.reshape(rows // 16, 8, FA) for v in (real_row, imag_row)]
                    at = (slot * 2 + c3) * FA
                    out[0, :, e1, :, at : at + FA] = jnp.concatenate(both, axis=1).astype(BF16)


def beam_factors(place, gains, packed, beams, own_pulses):
    rows = packed.shape[0]
    pulses = beams * own_pulses
    chips = beams // 2
    mixing = np.zeros((2, FA, FA), ml_dtypes.bfloat16)
    for core, c2, chip, c1, p, i in np.ndindex(2, 2, chips, 2, own_pulses, 2):
        lane = (((c2 * chips + chip) * 2 + c1) * own_pulses + p) * 2 + i
        mixing[core, i * pulses + (chip * 2 + core) * own_pulses + p, lane] = -1 if i else 1
    shape = jax.ShapeDtypeStruct((4, chips, 2, 16, 4 * FA), BF16)
    spec = pl.BlockSpec((1, chips, 2, 16, 4 * FA), lambda g: (g, 0, 0, 0, 0))
    def kernel(*refs):
        beam_kernel(2 * pulses, *refs)

    return pl.pallas_call(
        kernel,
        grid=(4,),
        out_shape=(shape, shape),
        in_specs=[SMEM, SMEM, VMEM, VMEM],
        out_specs=(spec, spec),
        compiler_params=pltpu.CompilerParams(vmem_limit_bytes=32 * 2**20),
        cost_estimate=pl.CostEstimate(flops=10**6, bytes_accessed=10**5, transcendentals=0),
    )(place, gains, packed, jnp.asarray(mixing))


def local(echoes, matched_filter, steering, kernels, blend_gains, beam_taps):
    zh = lax.axis_index("zh")
    zl = lax.axis_index("zl")
    own_rows = steering.shape[1]
    pulses = steering.shape[2]
    own_pulses = echoes.shape[1]
    beams = pulses // own_pulses
    slices = 4 * beams // 2
    core = lax.axis_index("core")
    place = ((zh * 4 + zl) * 2 + core).astype(jnp.int32).reshape(1)
    swap = [(0, 1), (1, 0)]
    tables = [jnp.asarray(table) for table in dft_blocks()]
    blocks = (2 * own_pulses, 2, FA, FA)

    far_echoes = lax.ppermute(echoes, "zh", swap)
    message, filters = compress_own(
        place, steering, beam_taps, echoes.reshape(blocks), matched_filter, kernels, tables, slices
    )
    far_message = compress_far(place, far_echoes.reshape(blocks), filters, kernels, tables, slices)
    arrived = lax.all_to_all(message, ("zl", "chip"), 0, 0, tiled=True)
    far_message, arrived = lax.optimization_barrier((far_message, arrived))
    far_own = lax.all_to_all(far_message, ("zl", "chip"), 0, 0, tiled=True)

    arrived = arrived.reshape(-1, arrived.shape[2])
    swapped = lax.ppermute(arrived, "core", swap)
    split_at = arrived.shape[1] - FA
    chips = beams // 2

    lanes = [v[: chips * own_rows, split_at:].reshape(chips, own_rows, FA) for v in (arrived, swapped)]
    lanes = jnp.where(core == 0, jnp.stack(lanes, axis=1), jnp.stack(lanes[::-1], axis=1))
    lanes = lanes.reshape(beams, own_rows, FA)
    taps = lanes[:, :, 2 * pulses : 2 * pulses + 2 * own_rows].reshape(beams, 2 * LEVELS, 2, own_rows)
    taps = jnp.transpose(taps, (0, 3, 1, 2)).reshape(beams, own_rows, 4 * LEVELS)
    packed = jnp.concatenate([lanes[:, :, : 2 * pulses], taps], axis=2)
    packed = jnp.pad(packed, ((0, 0), (0, 0), (0, FA - packed.shape[2])))
    near, far = beam_factors(
        place, blend_gains.reshape(-1), packed.reshape(-1, FA), beams, own_pulses
    )
    near, far = (v.reshape(-1, 4 * FA) for v in (near, far))
    total = dot(near[:, : 2 * FA], arrived[:, :split_at]) + dot(near[:, 2 * FA :], swapped[:, :split_at])

    far_own, total, far = lax.optimization_barrier((far_own.reshape(-1, split_at), total, far))
    far_swapped = lax.ppermute(far_own, "core", swap)
    total = total + dot(far[:, : 2 * FA], far_own)
    total = total + dot(far[:, 2 * FA :], far_swapped)
    result = total.astype(BF16).reshape(slices, 4 * own_rows, -1)
    arrived = lax.all_to_all(result, ("zl", "chip"), 0, 0, tiled=True)
    arrived = arrived.reshape(slices, 2, 2, own_rows, -1, FA)
    return jnp.transpose(arrived, (1, 3, 2, 4, 0, 5)).reshape(2, own_rows, 2, -1)


def solution(mesh):
    fine = Mesh(mesh.devices.reshape(4, 2, 4, 8, 2), ("g", "zh", "zl", "chip", "core"))
    sub = ("g", "zh", "zl")
    beam = ("chip", "core")
    return jax.shard_map(
        local,
        mesh=fine,
        in_specs=(
            P(sub, beam, None, None),
            P(),
            P(None, beam, None),
            P(),
            P(),
            P(None, None, None, beam),
        ),
        out_specs=P(sub, beam, None, None),
        check_vma=False,
    )
```

```python
import math

import jax
import jax.numpy as jnp
import ml_dtypes
import numpy as np
from jax import lax
from jax.experimental import pallas as pl
from jax.experimental.pallas import tpu as pltpu
from jax.sharding import Mesh
from jax.sharding import PartitionSpec as P

FA = 128
LEVELS = 4
BF16 = jnp.bfloat16
F32 = jnp.float32


def halves(table):
    high = table.astype(ml_dtypes.bfloat16)
    low = (table - high.astype(np.float64)).astype(ml_dtypes.bfloat16)
    return np.stack([high, low])


def dft_blocks():
    index = np.arange(FA)
    product = index[:, None] * index[None, :]
    angle = (product % FA) * (2.0 * math.pi / FA)
    c, s = np.cos(angle), np.sin(angle)
    turn = (product % (FA * FA)) * (2.0 * math.pi / (FA * FA))
    return (
        halves(np.block([[c, s], [-s, c]])),
        halves(np.block([[c, -s], [s, c]])),
        np.stack([np.cos(turn), np.sin(turn)]).astype(np.float32),
    )


def split(value):
    high = value.astype(BF16)
    return high, (value - high.astype(F32)).astype(BF16)


def dot(left, right):
    return jnp.dot(left, right, preferred_element_type=F32)


def dot_table(value, table):
    high, low = split(value)
    return dot(high, table[0]) + dot(low, table[0]) + dot(high, table[1])


def table_dot(table, value):
    high, low = split(value)
    return dot(table[0], high) + dot(table[0], low) + dot(table[1], high)


def complex_block(ref, *index):
    real_part, imag_part = ref[(*index, 0)], ref[(*index, 1)]
    top = jnp.concatenate([real_part, imag_part], axis=1)
    return jnp.concatenate([top, jnp.concatenate([-imag_part, real_part], axis=1)], axis=0)


def place_bits(place):
    value = place[0]
    return (value >> 1) & 1, (value >> 2) & 1, (value >> 3) & 1, value & 1


def range_matrices(bits, kern):
    chain = complex_block(kern, 3, bits[2]).astype(F32)
    for level in (2, 1):
        high, low = split(chain)
        block = complex_block(kern, level, bits[level - 1])
        chain = dot(block, high) + dot(block, low)
    high, low = split(chain)
    mats = []
    for child in range(2):
        block = complex_block(kern, 0, child)
        mats.append((dot(block, high) + dot(block, low)).astype(BF16))
    return mats


def forward_left(echo, plus, turn):
    count = echo.shape[0]
    c, s = turn[0], turn[1]
    signal = jnp.concatenate([echo[q].reshape(2 * FA, FA) for q in range(count)], axis=1)
    first = dot(plus[0], signal) + dot(plus[1], signal)
    stacked = []
    for q in range(count):
        real_part = first[:FA, q * FA : (q + 1) * FA]
        imag_part = first[FA:, q * FA : (q + 1) * FA]
        stacked.append(
            jnp.concatenate([real_part * c + imag_part * s, imag_part * c - real_part * s], axis=1)
        )
    return jnp.concatenate(stacked, axis=0)


def filtered(spectrum, filters):
    stacked = []
    for q in range(spectrum.shape[0] // FA):
        real_part = spectrum[q * FA : (q + 1) * FA, :FA]
        imag_part = spectrum[q * FA : (q + 1) * FA, FA:]
        stacked.append(
            jnp.concatenate(
                [
                    real_part * filters[0] - imag_part * filters[1],
                    real_part * filters[1] + imag_part * filters[0],
                ],
                axis=1,
            )
        )
    return jnp.concatenate(stacked, axis=0)


def inverse_left(back, minus, turn):
    c, s = turn[0], turn[1]
    stacked = []
    for q in range(back.shape[0] // FA):
        real_part = back[q * FA : (q + 1) * FA, :FA]
        imag_part = back[q * FA : (q + 1) * FA, FA:]
        stacked.append(
            jnp.concatenate([real_part * c - imag_part * s, imag_part * c + real_part * s], axis=0)
        )
    return table_dot(minus, jnp.concatenate(stacked, axis=1)).astype(BF16)


def times_range(pulses, mats, rows):
    count = pulses.shape[1] // FA
    for q in range(count):
        lanes = slice(q * FA, (q + 1) * FA)
        pair = jnp.concatenate([pulses[:FA, lanes], pulses[FA:, lanes]], axis=1)
        turned = dot(pair, mats[q * 2 // count])
        rows[pl.ds(2 * q, FA, stride=2 * count), :] = turned[:, :FA]
        rows[pl.ds(2 * q + 1, FA, stride=2 * count), :] = turned[:, FA:]


def send_order(rows, out):
    copies, slices, width = out.shape[:3]
    for part in range(FA // slices):
        piece = rows[pl.ds(part * slices * width, slices * width), :]
        piece = piece.reshape(slices, width, FA).astype(BF16)
        for copy in range(copies):
            out[copy, :, :, part * FA : (part + 1) * FA] = piece


def own_kernel(place, echo_hbm, matched_hbm, kern_hbm, plus_hbm, minus_hbm, turn_hbm, out, *refs):
    echo, matched, kern, plus, minus, turn, lines, rows, sems = refs
    loads = [
        pltpu.make_async_copy(source, target, sems.at[at])
        for at, (source, target) in enumerate(
            (
                (kern_hbm, kern),
                (plus_hbm, plus),
                (echo_hbm, echo),
                (turn_hbm, turn),
                (minus_hbm, minus),
                (matched_hbm, matched),
            )
        )
    ]
    for load in loads:
        load.start()
    loads[0].wait()
    mats = range_matrices(place_bits(place), kern)
    for load in loads[1:4]:
        load.wait()
    turned = forward_left(echo, plus, turn)
    loads[4].wait()
    spectrum = dot_table(turned, minus)
    loads[5].wait()
    for j in range(FA):
        lines[0, j : j + 1, :] = matched[0:1, j * FA : (j + 1) * FA]
        lines[1, j : j + 1, :] = matched[1:2, j * FA : (j + 1) * FA]
    scale = 1.0 / (FA * FA)
    filters = [jnp.transpose(lines[part]) * scale for part in range(2)]
    back = dot_table(filtered(spectrum, filters), plus)
    times_range(inverse_left(back, minus, turn), mats, rows)
    send_order(rows, out)


SMEM = pl.BlockSpec(memory_space=pltpu.SMEM)
VMEM = pl.BlockSpec(memory_space=pltpu.VMEM)
ANY = pl.BlockSpec(memory_space=pl.ANY)


def compress_own(place, echo, matched, kern, tables, copies, slices):
    large = [echo, matched, kern, *tables]
    width = 2 * echo.shape[0]
    return pl.pallas_call(
        own_kernel,
        out_shape=jax.ShapeDtypeStruct((copies, slices, width, FA * FA // slices), BF16),
        in_specs=[SMEM] + [ANY] * len(large),
        out_specs=VMEM,
        scratch_shapes=[pltpu.VMEM(table.shape, table.dtype) for table in large]
        + [
            pltpu.VMEM((2, FA, FA), F32),
            pltpu.VMEM((FA * width, FA), F32),
            pltpu.SemaphoreType.DMA((len(large),)),
        ],
        compiler_params=pltpu.CompilerParams(vmem_limit_bytes=60 * 2**20),
        cost_estimate=pl.CostEstimate(flops=10**9, bytes_accessed=2 * 10**6, transcendentals=0),
    )(place, *large)


def beam_kernel(steer_lanes, place, gains, packed, mixing, out_own, out_other):
    e3 = pl.program_id(0) // 2
    e2 = pl.program_id(0) % 2
    _, _, e4, core = place_bits(place)
    rows = packed.shape[0]
    data = packed[...]
    taps = data.astype(F32)
    row = lax.broadcasted_iota(jnp.int32, (rows, FA), 0)
    lane = lax.broadcasted_iota(jnp.int32, (rows, FA), 1)

    def weights(level, child, parity):
        at = steer_lanes + (level * 2 + child) * 2
        even, odd = taps[:, at : at + 1], taps[:, at + 1 : at + 2]
        if isinstance(parity, int):
            tap = odd if parity else even
        else:
            tap = jnp.where(parity == 1, odd, even)
        tap = jnp.broadcast_to(tap, (rows, FA))
        index = ((level * 2 + child) * 2 + parity) * 2
        g0, g1 = gains[index], gains[index + 1]
        backward = tap < 0
        before = jnp.where(backward & (row > 0), g0, 0.0)
        here = jnp.where(backward, g1, g0)
        after = jnp.where(jnp.logical_not(backward) & (row < rows - 1), g1, 0.0)
        return before, here, after

    def by_lane(level, parity, second):
        pair = [weights(level, child, parity) for child in range(2)]
        return [jnp.where(second, odd, even) for even, odd in zip(*pair)]

    def neighbours(value):
        return pltpu.roll(value, 1, 0), value, pltpu.roll(value, rows - 1, 0)

    def blend(near, weight):
        return near[0] * weight[0] + near[1] * weight[1] + near[2] * weight[2]

    def of_core(value):
        tiles = value.reshape(rows // 16, 2, 8, FA)
        return jnp.where(core == 0, tiles[:, 0], tiles[:, 1]).reshape(rows // 2, FA)

    level2 = by_lane(1, e2, lane >= FA // 2)
    level3 = [weights(2, child, e3) for child in range(2)]
    level4 = [[of_core(w) for w in weights(3, child, e4)] for child in range(2)]
    imaginary = lane[: rows // 2] % 2 == 1
    for e1 in range(2):
        level1 = by_lane(0, e1, (lane // 4) % 2 == 1)
        for slot, out in ((0, out_own), (1, out_other)):
            source = jnp.where(slot == 0, core, 1 - core)
            second = blend(neighbours(dot(data, mixing[source])), level1)
            second = neighbours(blend(neighbours(second), level2))
            for c3 in range(2):
                third = [of_core(v) for v in neighbours(blend(second, level3[c3]))]
                for c4 in range(2):
                    real_row = blend(third, level4[c4])
                    imag_row = jnp.where(
                        imaginary, pltpu.roll(real_row, 1, 1), -pltpu.roll(real_row, FA - 1, 1)
                    )
                    both = [v.reshape(rows // 16, 8, FA) for v in (real_row, imag_row)]
                    at = (c4 * 2 + c3) * FA
                    out[0, :, e1, :, at : at + FA] = jnp.concatenate(both, axis=1).astype(BF16)


def beam_factors(place, gains, packed, beams, own_pulses):
    rows = packed.shape[0]
    pulses = beams * own_pulses
    chips = beams // 2
    mixing = np.zeros((2, FA, FA), ml_dtypes.bfloat16)
    for core, c2, chip, c1, p, i in np.ndindex(2, 2, chips, 2, own_pulses, 2):
        lane = (((c2 * chips + chip) * 2 + c1) * own_pulses + p) * 2 + i
        mixing[core, i * pulses + (chip * 2 + core) * own_pulses + p, lane] = -1 if i else 1
    shape = jax.ShapeDtypeStruct((4, chips, 2, 16, 4 * FA), BF16)
    spec = pl.BlockSpec((1, chips, 2, 16, 4 * FA), lambda g: (g, 0, 0, 0, 0))
    def kernel(*refs):
        beam_kernel(2 * pulses, *refs)

    return pl.pallas_call(
        kernel,
        grid=(4,),
        out_shape=(shape, shape),
        in_specs=[SMEM, SMEM, VMEM, VMEM],
        out_specs=(spec, spec),
        compiler_params=pltpu.CompilerParams(vmem_limit_bytes=32 * 2**20),
        cost_estimate=pl.CostEstimate(flops=10**6, bytes_accessed=10**5, transcendentals=0),
    )(place, gains, packed, jnp.asarray(mixing))


def gather_rows(packed, core, chip):
    steps = [("core", 1, core)] + [("chip", 1 << bit, (chip >> bit) & 1) for bit in range(3)]
    for axis, apart, upper in steps:
        size = lax.axis_size(axis)
        got = lax.ppermute(packed, axis, [(i, i ^ apart) for i in range(size)])
        low, high = jnp.where(upper == 0, packed, got), jnp.where(upper == 0, got, packed)
        packed = jnp.concatenate([low, high], axis=0)
    return packed


def local(echoes, matched_filter, steering, kernels, blend_gains, beam_taps):
    zh = lax.axis_index("zh")
    zl = lax.axis_index("zl")
    core = lax.axis_index("core")
    own_rows = steering.shape[1]
    pulses = steering.shape[2]
    own_pulses = echoes.shape[1]
    beams = pulses // own_pulses
    slices = 4 * beams // 2
    place = ((zh * 4 + zl) * 2 + core).astype(jnp.int32).reshape(1)
    tables = [jnp.asarray(table) for table in dft_blocks()]

    message = compress_own(
        place, echoes.reshape(2 * own_pulses, 2, FA, FA), matched_filter, kernels, tables, 2, slices
    )
    message, steering, beam_taps = lax.optimization_barrier((message, steering, beam_taps))
    width = message.shape[2]
    own = lax.all_to_all(
        message.reshape(2 * slices, width, -1), ("zh", "zl", "chip"), 0, 0, tiled=True
    ).reshape(2 * slices * width, -1)

    packed = jnp.concatenate(
        [
            jnp.moveaxis(steering, 1, 0).reshape(own_rows, 2 * pulses),
            jnp.moveaxis(beam_taps, 3, 0).reshape(own_rows, 4 * LEVELS).astype(BF16),
        ],
        axis=1,
    )
    packed = jnp.pad(packed, ((0, 0), (0, FA - packed.shape[1])))
    packed = gather_rows(packed, core, lax.axis_index("chip"))
    near, far = beam_factors(place, blend_gains.reshape(-1), packed, beams, own_pulses)

    own, near, far = lax.optimization_barrier((own, near, far))
    other = lax.ppermute(own, "core", [(0, 1), (1, 0)])
    total = dot(near.reshape(-1, 4 * FA), own)
    total = total + dot(far.reshape(-1, 4 * FA), other)
    result = total.astype(BF16).reshape(slices, 4 * own_rows, -1)
    arrived = lax.all_to_all(result, ("zl", "chip"), 0, 0, tiled=True)
    arrived = arrived.reshape(slices, 2, 2, own_rows, -1, FA)
    return jnp.transpose(arrived, (1, 3, 2, 4, 0, 5)).reshape(2, own_rows, 2, -1)


def solution(mesh):
    fine = Mesh(mesh.devices.reshape(4, 2, 4, 8, 2), ("g", "zh", "zl", "chip", "core"))
    sub = ("g", "zh", "zl")
    beam = ("chip", "core")
    return jax.shard_map(
        local,
        mesh=fine,
        in_specs=(
            P(sub, beam, None, None),
            P(),
            P(None, beam, None),
            P(),
            P(),
            P(None, None, None, beam),
        ),
        out_specs=P(sub, beam, None, None),
        check_vma=False,
    )
```

```python
import math

import jax
import jax.numpy as jnp
import ml_dtypes
import numpy as np
from jax import lax
from jax.experimental import pallas as pl
from jax.experimental.pallas import tpu as pltpu
from jax.sharding import Mesh
from jax.sharding import PartitionSpec as P

FA = 128
LEVELS = 4
BF16 = jnp.bfloat16
F32 = jnp.float32


def halves(table):
    high = table.astype(ml_dtypes.bfloat16)
    low = (table - high.astype(np.float64)).astype(ml_dtypes.bfloat16)
    return np.stack([high, low])


def dft_blocks():
    index = np.arange(FA)
    product = index[:, None] * index[None, :]
    angle = (product % FA) * (2.0 * math.pi / FA)
    c, s = np.cos(angle), np.sin(angle)
    turn = (product % (FA * FA)) * (2.0 * math.pi / (FA * FA))
    return (
        halves(np.block([[c, s], [-s, c]])),
        halves(np.block([[c, -s], [s, c]])),
        np.stack([np.cos(turn), np.sin(turn)]).astype(np.float32),
    )


def split(value):
    high = value.astype(BF16)
    return high, (value - high.astype(F32)).astype(BF16)


def dot(left, right):
    return jnp.dot(left, right, preferred_element_type=F32)


def dot_table(value, table):
    high, low = split(value)
    return dot(high, table[0]) + dot(low, table[0]) + dot(high, table[1])


def table_dot(table, value):
    high, low = split(value)
    return dot(table[0], high) + dot(table[0], low) + dot(table[1], high)


def complex_block(ref, *index):
    real_part, imag_part = ref[(*index, 0)], ref[(*index, 1)]
    top = jnp.concatenate([real_part, imag_part], axis=1)
    return jnp.concatenate([top, jnp.concatenate([-imag_part, real_part], axis=1)], axis=0)


def place_bits(place):
    value = place[0]
    return (value >> 1) & 1, (value >> 2) & 1, (value >> 3) & 1, value & 1


def range_matrices(bits, kern):
    chain = complex_block(kern, 3, bits[2]).astype(F32)
    for level in (2, 1):
        high, low = split(chain)
        block = complex_block(kern, level, bits[level - 1])
        chain = dot(block, high) + dot(block, low)
    high, low = split(chain)
    mats = []
    for child in range(2):
        block = complex_block(kern, 0, child)
        mats.append((dot(block, high) + dot(block, low)).astype(BF16))
    return mats


def forward_left(signal, plus, turn):
    count = signal.shape[1] // FA
    c, s = turn[0], turn[1]
    first = dot(plus[0], signal) + dot(plus[1], signal)
    stacked = []
    for q in range(count):
        real_part = first[:FA, q * FA : (q + 1) * FA]
        imag_part = first[FA:, q * FA : (q + 1) * FA]
        stacked.append(
            jnp.concatenate([real_part * c + imag_part * s, imag_part * c - real_part * s], axis=1)
        )
    return jnp.concatenate(stacked, axis=0)


def filtered(spectrum, filters):
    stacked = []
    for q in range(spectrum.shape[0] // FA):
        real_part = spectrum[q * FA : (q + 1) * FA, :FA]
        imag_part = spectrum[q * FA : (q + 1) * FA, FA:]
        stacked.append(
            jnp.concatenate(
                [
                    real_part * filters[0] - imag_part * filters[1],
                    real_part * filters[1] + imag_part * filters[0],
                ],
                axis=1,
            )
        )
    return jnp.concatenate(stacked, axis=0)


def inverse_left(back, minus, turn):
    c, s = turn[0], turn[1]
    stacked = []
    for q in range(back.shape[0] // FA):
        real_part = back[q * FA : (q + 1) * FA, :FA]
        imag_part = back[q * FA : (q + 1) * FA, FA:]
        stacked.append(
            jnp.concatenate([real_part * c - imag_part * s, imag_part * c + real_part * s], axis=0)
        )
    return table_dot(minus, jnp.concatenate(stacked, axis=1)).astype(BF16)


def times_range(pulses, mats, rows):
    count = pulses.shape[1] // FA
    for q in range(count):
        lanes = slice(q * FA, (q + 1) * FA)
        pair = jnp.concatenate([pulses[:FA, lanes], pulses[FA:, lanes]], axis=1)
        turned = dot(pair, mats[q * 2 // count])
        rows[pl.ds(2 * q, FA, stride=2 * count), :] = turned[:, :FA]
        rows[pl.ds(2 * q + 1, FA, stride=2 * count), :] = turned[:, FA:]


def send_order(rows, out):
    slices, copies, width = out.shape[:3]
    for part in range(FA // slices):
        piece = rows[pl.ds(part * slices * width, slices * width), :]
        piece = piece.reshape(slices, width, FA).astype(BF16)
        for copy in range(copies):
            out[:, copy, :, part * FA : (part + 1) * FA] = piece


def own_kernel(place, echo_hbm, matched_hbm, kern_hbm, plus_hbm, minus_hbm, turn_hbm, out, *refs):
    echo, matched, kern, plus, minus, turn, signal, lines, rows, sems = refs
    loads = [
        pltpu.make_async_copy(source, target, sems.at[at])
        for at, (source, target) in enumerate(
            (
                (echo_hbm, echo),
                (plus_hbm, plus),
                (turn_hbm, turn),
                (kern_hbm, kern),
                (minus_hbm, minus),
                (matched_hbm, matched),
            )
        )
    ]
    for load in loads:
        load.start()
    loads[0].wait()
    pulses = echo.shape[1]
    for n in range(FA):
        for q in range(echo.shape[0] * pulses):
            pair = echo[q // pulses, q % pulses, :, n * FA : (n + 1) * FA].astype(F32)
            signal[n : n + 1, q * FA : (q + 1) * FA] = pair[0:1]
            signal[FA + n : FA + n + 1, q * FA : (q + 1) * FA] = pair[1:2]
    for load in loads[1:]:
        load.wait()
    mats = range_matrices(place_bits(place), kern)
    turned = forward_left(signal[...].astype(BF16), plus, turn)
    spectrum = dot_table(turned, minus)
    for j in range(FA):
        lines[0, j : j + 1, :] = matched[0:1, j * FA : (j + 1) * FA]
        lines[1, j : j + 1, :] = matched[1:2, j * FA : (j + 1) * FA]
    scale = 1.0 / (FA * FA)
    filters = [jnp.transpose(lines[part]) * scale for part in range(2)]
    back = dot_table(filtered(spectrum, filters), plus)
    times_range(inverse_left(back, minus, turn), mats, rows)
    send_order(rows, out)


SMEM = pl.BlockSpec(memory_space=pltpu.SMEM)
VMEM = pl.BlockSpec(memory_space=pltpu.VMEM)
ANY = pl.BlockSpec(memory_space=pl.ANY)


def compress_own(place, echo, matched, kern, tables, copies, slices):
    large = [echo, matched, kern, *tables]
    width = 2 * echo.shape[0] * echo.shape[1]
    return pl.pallas_call(
        own_kernel,
        out_shape=jax.ShapeDtypeStruct((slices, copies, width, FA * FA // slices), BF16),
        in_specs=[SMEM] + [ANY] * len(large),
        out_specs=VMEM,
        scratch_shapes=[pltpu.VMEM(table.shape, table.dtype) for table in large]
        + [
            pltpu.VMEM((2 * FA, width // 2 * FA), F32),
            pltpu.VMEM((2, FA, FA), F32),
            pltpu.VMEM((FA * width, FA), F32),
            pltpu.SemaphoreType.DMA((len(large),)),
        ],
        compiler_params=pltpu.CompilerParams(vmem_limit_bytes=60 * 2**20),
        cost_estimate=pl.CostEstimate(flops=10**9, bytes_accessed=2 * 10**6, transcendentals=0),
    )(place, *large)


def beam_kernel(steer_lanes, place, gains, packed, mixing, out_own, out_other):
    e3 = pl.program_id(0) // 2
    e2 = pl.program_id(0) % 2
    _, _, e4, core = place_bits(place)
    rows = packed.shape[0]
    data = packed[...]
    taps = data.astype(F32)
    row = lax.broadcasted_iota(jnp.int32, (rows, FA), 0)
    lane = lax.broadcasted_iota(jnp.int32, (rows, FA), 1)

    def weights(level, child, parity):
        at = steer_lanes + (level * 2 + child) * 2
        even, odd = taps[:, at : at + 1], taps[:, at + 1 : at + 2]
        if isinstance(parity, int):
            tap = odd if parity else even
        else:
            tap = jnp.where(parity == 1, odd, even)
        tap = jnp.broadcast_to(tap, (rows, FA))
        index = ((level * 2 + child) * 2 + parity) * 2
        g0, g1 = gains[index], gains[index + 1]
        backward = tap < 0
        before = jnp.where(backward & (row > 0), g0, 0.0)
        here = jnp.where(backward, g1, g0)
        after = jnp.where(jnp.logical_not(backward) & (row < rows - 1), g1, 0.0)
        return before, here, after

    def by_lane(level, parity, second):
        pair = [weights(level, child, parity) for child in range(2)]
        return [jnp.where(second, odd, even) for even, odd in zip(*pair)]

    def neighbours(value):
        return pltpu.roll(value, 1, 0), value, pltpu.roll(value, rows - 1, 0)

    def blend(near, weight):
        return near[0] * weight[0] + near[1] * weight[1] + near[2] * weight[2]

    def of_core(value):
        tiles = value.reshape(rows // 16, 2, 8, FA)
        return jnp.where(core == 0, tiles[:, 0], tiles[:, 1]).reshape(rows // 2, FA)

    level2 = [weights(1, child, e2) for child in range(2)]
    level3 = [weights(2, child, e3) for child in range(2)]
    level4 = [of_core(w) for w in by_lane(3, e4, (lane // 8) % 2 == 1)]
    imaginary = lane[: rows // 2] % 2 == 1
    for e1 in range(2):
        level1 = by_lane(0, e1, (lane // 4) % 2 == 1)
        for slot, out in ((0, out_own), (1, out_other)):
            source = jnp.where(slot == 0, core, 1 - core)
            first = neighbours(blend(neighbours(dot(data, mixing[source])), level1))
            for c2 in range(2):
                second = neighbours(blend(first, level2[c2]))
                for c3 in range(2):
                    third = [of_core(v) for v in neighbours(blend(second, level3[c3]))]
                    real_row = blend(third, level4)
                    imag_row = jnp.where(
                        imaginary, pltpu.roll(real_row, 1, 1), -pltpu.roll(real_row, FA - 1, 1)
                    )
                    both = [v.reshape(rows // 16, 8, FA) for v in (real_row, imag_row)]
                    at = (c3 * 2 + c2) * FA
                    out[0, :, e1, :, at : at + FA] = jnp.concatenate(both, axis=1).astype(BF16)


def beam_factors(place, gains, packed, beams, own_pulses):
    rows = packed.shape[0]
    pulses = beams * own_pulses
    chips = beams // 2
    mixing = np.zeros((2, FA, FA), ml_dtypes.bfloat16)
    for core, chip, c4, c1, p, i in np.ndindex(2, chips, 2, 2, own_pulses, 2):
        lane = (((chip * 2 + c4) * 2 + c1) * own_pulses + p) * 2 + i
        mixing[core, i * pulses + (chip * 2 + core) * own_pulses + p, lane] = -1 if i else 1
    shape = jax.ShapeDtypeStruct((4, chips, 2, 16, 4 * FA), BF16)
    spec = pl.BlockSpec((1, chips, 2, 16, 4 * FA), lambda g: (g, 0, 0, 0, 0))
    def kernel(*refs):
        beam_kernel(2 * pulses, *refs)

    return pl.pallas_call(
        kernel,
        grid=(4,),
        out_shape=(shape, shape),
        in_specs=[SMEM, SMEM, VMEM, VMEM],
        out_specs=(spec, spec),
        compiler_params=pltpu.CompilerParams(vmem_limit_bytes=32 * 2**20),
        cost_estimate=pl.CostEstimate(flops=10**6, bytes_accessed=10**5, transcendentals=0),
    )(place, gains, packed, jnp.asarray(mixing))


def gather_rows(packed, core, chip):
    steps = [("core", 1, core)] + [("chip", 1 << bit, (chip >> bit) & 1) for bit in range(3)]
    for axis, apart, upper in steps:
        size = lax.axis_size(axis)
        got = lax.ppermute(packed, axis, [(i, i ^ apart) for i in range(size)])
        low, high = jnp.where(upper == 0, packed, got), jnp.where(upper == 0, got, packed)
        packed = jnp.concatenate([low, high], axis=0)
    return packed


def local(echoes, matched_filter, steering, kernels, blend_gains, beam_taps):
    zh = lax.axis_index("zh")
    zl = lax.axis_index("zl")
    core = lax.axis_index("core")
    own_rows = steering.shape[1]
    pulses = steering.shape[2]
    own_pulses = echoes.shape[1]
    beams = pulses // own_pulses
    slices = 4 * beams // 2
    place = ((zh * 4 + zl) * 2 + core).astype(jnp.int32).reshape(1)
    tables = [jnp.asarray(table) for table in dft_blocks()]

    message = compress_own(
        place, echoes, matched_filter, kernels, tables, 2, slices
    )
    message, steering, beam_taps = lax.optimization_barrier((message, steering, beam_taps))
    width = message.shape[2]
    own = lax.all_to_all(
        message.reshape(2 * slices, width, -1), ("zl", "chip", "zh"), 0, 0, tiled=True
    ).reshape(2 * slices * width, -1)

    packed = jnp.concatenate(
        [
            jnp.moveaxis(steering, 1, 0).reshape(own_rows, 2 * pulses),
            jnp.moveaxis(beam_taps, 3, 0).reshape(own_rows, 4 * LEVELS).astype(BF16),
        ],
        axis=1,
    )
    packed = jnp.pad(packed, ((0, 0), (0, FA - packed.shape[1])))
    packed = gather_rows(packed, core, lax.axis_index("chip"))
    near, far = beam_factors(place, blend_gains.reshape(-1), packed, beams, own_pulses)

    own, near, far = lax.optimization_barrier((own, near, far))
    other = lax.ppermute(own, "core", [(0, 1), (1, 0)])
    total = dot(near.reshape(-1, 4 * FA), own)
    total = total + dot(far.reshape(-1, 4 * FA), other)
    result = total.astype(BF16).reshape(slices, 4 * own_rows, -1)
    arrived = lax.all_to_all(result, ("zl", "chip"), 0, 0, tiled=True)
    arrived = arrived.reshape(slices, 2, 2, own_rows, -1, FA)
    return jnp.transpose(arrived, (1, 3, 2, 4, 0, 5)).reshape(2, own_rows, 2, -1)


def solution(mesh):
    fine = Mesh(mesh.devices.reshape(4, 2, 4, 8, 2), ("g", "zh", "zl", "chip", "core"))
    sub = ("g", "zh", "zl")
    beam = ("chip", "core")
    return jax.shard_map(
        local,
        mesh=fine,
        in_specs=(
            P(sub, beam, None, None),
            P(),
            P(None, beam, None),
            P(),
            P(),
            P(None, None, None, beam),
        ),
        out_specs=P(sub, beam, None, None),
        check_vma=False,
    )
```

```python
import math

import jax
import jax.numpy as jnp
import ml_dtypes
import numpy as np
from jax import lax
from jax.experimental import pallas as pl
from jax.experimental.pallas import tpu as pltpu
from jax.sharding import Mesh
from jax.sharding import PartitionSpec as P

FA = 128
LEVELS = 4
BF16 = jnp.bfloat16
F32 = jnp.float32


def halves(table):
    high = table.astype(ml_dtypes.bfloat16)
    low = (table - high.astype(np.float64)).astype(ml_dtypes.bfloat16)
    return np.stack([high, low])


def dft_blocks():
    index = np.arange(FA)
    product = index[:, None] * index[None, :]
    angle = (product % FA) * (2.0 * math.pi / FA)
    c, s = np.cos(angle), np.sin(angle)
    turn = (product % (FA * FA)) * (2.0 * math.pi / (FA * FA))
    return (
        halves(np.block([[c, s], [-s, c]])),
        halves(np.block([[c, -s], [s, c]])),
        np.stack([np.cos(turn), np.sin(turn)]).astype(np.float32),
    )


def split(value):
    high = value.astype(BF16)
    return high, (value - high.astype(F32)).astype(BF16)


def dot(left, right):
    return jnp.dot(left, right, preferred_element_type=F32)


def dot_table(value, table):
    high, low = split(value)
    return dot(high, table[0]) + dot(low, table[0]) + dot(high, table[1])


def table_dot(table, value):
    high, low = split(value)
    return dot(table[0], high) + dot(table[0], low) + dot(table[1], high)


def complex_block(ref, *index):
    real_part, imag_part = ref[(*index, 0)], ref[(*index, 1)]
    top = jnp.concatenate([real_part, imag_part], axis=1)
    return jnp.concatenate([top, jnp.concatenate([-imag_part, real_part], axis=1)], axis=0)


def place_bits(place):
    value = place[0]
    return (value >> 1) & 1, (value >> 2) & 1, (value >> 3) & 1, value & 1


def range_matrices(bits, kern):
    chain = complex_block(kern, 3, bits[2]).astype(F32)
    for level in (2, 1):
        high, low = split(chain)
        block = complex_block(kern, level, bits[level - 1])
        chain = dot(block, high) + dot(block, low)
    high, low = split(chain)
    mats = []
    for child in range(2):
        block = complex_block(kern, 0, child)
        mats.append((dot(block, high) + dot(block, low)).astype(BF16))
    return mats


def forward_left(signal, plus, turn):
    count = signal.shape[1] // FA
    c, s = turn[0], turn[1]
    first = dot(plus[0], signal) + dot(plus[1], signal)
    stacked = []
    for q in range(count):
        real_part = first[:FA, q * FA : (q + 1) * FA]
        imag_part = first[FA:, q * FA : (q + 1) * FA]
        stacked.append(
            jnp.concatenate([real_part * c + imag_part * s, imag_part * c - real_part * s], axis=1)
        )
    return jnp.concatenate(stacked, axis=0)


def filtered(spectrum, filters):
    stacked = []
    for q in range(spectrum.shape[0] // FA):
        real_part = spectrum[q * FA : (q + 1) * FA, :FA]
        imag_part = spectrum[q * FA : (q + 1) * FA, FA:]
        stacked.append(
            jnp.concatenate(
                [
                    real_part * filters[0] - imag_part * filters[1],
                    real_part * filters[1] + imag_part * filters[0],
                ],
                axis=1,
            )
        )
    return jnp.concatenate(stacked, axis=0)


def inverse_left(back, minus, turn):
    c, s = turn[0], turn[1]
    stacked = []
    for q in range(back.shape[0] // FA):
        real_part = back[q * FA : (q + 1) * FA, :FA]
        imag_part = back[q * FA : (q + 1) * FA, FA:]
        stacked.append(
            jnp.concatenate([real_part * c - imag_part * s, imag_part * c + real_part * s], axis=0)
        )
    return table_dot(minus, jnp.concatenate(stacked, axis=1)).astype(BF16)


def times_range(pulses, mats, rows):
    count = pulses.shape[1] // FA
    for q in range(count):
        lanes = slice(q * FA, (q + 1) * FA)
        pair = jnp.concatenate([pulses[:FA, lanes], pulses[FA:, lanes]], axis=1)
        turned = dot(pair, mats[q * 2 // count])
        rows[pl.ds(2 * q, FA, stride=2 * count), :] = turned[:, :FA]
        rows[pl.ds(2 * q + 1, FA, stride=2 * count), :] = turned[:, FA:]


def send_order(rows, out):
    slices, copies, width = out.shape[:3]
    for part in range(FA // slices):
        piece = rows[pl.ds(part * slices * width, slices * width), :]
        piece = piece.reshape(slices, width, FA).astype(BF16)
        for copy in range(copies):
            out[:, copy, :, part * FA : (part + 1) * FA] = piece


def own_kernel(place, echo_hbm, matched_hbm, kern_hbm, plus_hbm, minus_hbm, turn_hbm, out, *refs):
    echo, matched, kern, plus, minus, turn, signal, lines, rows, sems = refs
    loads = [
        pltpu.make_async_copy(source, target, sems.at[at])
        for at, (source, target) in enumerate(
            (
                (echo_hbm, echo),
                (plus_hbm, plus),
                (turn_hbm, turn),
                (kern_hbm, kern),
                (minus_hbm, minus),
                (matched_hbm, matched),
            )
        )
    ]
    for load in loads:
        load.start()
    loads[0].wait()
    pulses = echo.shape[1]
    for n in range(FA):
        for q in range(echo.shape[0] * pulses):
            pair = echo[q // pulses, q % pulses, :, n * FA : (n + 1) * FA].astype(F32)
            signal[n : n + 1, q * FA : (q + 1) * FA] = pair[0:1]
            signal[FA + n : FA + n + 1, q * FA : (q + 1) * FA] = pair[1:2]
    for load in loads[1:]:
        load.wait()
    mats = range_matrices(place_bits(place), kern)
    turned = forward_left(signal[...].astype(BF16), plus, turn)
    spectrum = dot_table(turned, minus)
    for j in range(FA):
        lines[0, j : j + 1, :] = matched[0:1, j * FA : (j + 1) * FA]
        lines[1, j : j + 1, :] = matched[1:2, j * FA : (j + 1) * FA]
    scale = 1.0 / (FA * FA)
    filters = [jnp.transpose(lines[part]) * scale for part in range(2)]
    back = dot_table(filtered(spectrum, filters), plus)
    times_range(inverse_left(back, minus, turn), mats, rows)
    send_order(rows, out)


SMEM = pl.BlockSpec(memory_space=pltpu.SMEM)
VMEM = pl.BlockSpec(memory_space=pltpu.VMEM)
ANY = pl.BlockSpec(memory_space=pl.ANY)


def compress_own(place, echo, matched, kern, tables, copies, slices):
    large = [echo, matched, kern, *tables]
    width = 2 * echo.shape[0] * echo.shape[1]
    return pl.pallas_call(
        own_kernel,
        out_shape=jax.ShapeDtypeStruct((slices, copies, width, FA * FA // slices), BF16),
        in_specs=[SMEM] + [ANY] * len(large),
        out_specs=VMEM,
        scratch_shapes=[pltpu.VMEM(table.shape, table.dtype) for table in large]
        + [
            pltpu.VMEM((2 * FA, width // 2 * FA), F32),
            pltpu.VMEM((2, FA, FA), F32),
            pltpu.VMEM((FA * width, FA), F32),
            pltpu.SemaphoreType.DMA((len(large),)),
        ],
        compiler_params=pltpu.CompilerParams(vmem_limit_bytes=60 * 2**20),
        cost_estimate=pl.CostEstimate(flops=10**9, bytes_accessed=2 * 10**6, transcendentals=0),
    )(place, *large)


def beam_kernel(steer_lanes, place, gains, packed, mixing, out_own, out_other, firsts, seconds):
    e3 = pl.program_id(0) // 2
    e2 = pl.program_id(0) % 2
    _, _, e4, core = place_bits(place)
    rows = packed.shape[0]
    data = packed[...]
    taps = data.astype(F32)
    row = lax.broadcasted_iota(jnp.int32, (rows, FA), 0)
    lane = lax.broadcasted_iota(jnp.int32, (rows, FA), 1)

    def weights(level, child, parity):
        at = steer_lanes + (level * 2 + child) * 2
        even, odd = taps[:, at : at + 1], taps[:, at + 1 : at + 2]
        if isinstance(parity, int):
            tap = odd if parity else even
        else:
            tap = jnp.where(parity == 1, odd, even)
        tap = jnp.broadcast_to(tap, (rows, FA))
        index = ((level * 2 + child) * 2 + parity) * 2
        g0, g1 = gains[index], gains[index + 1]
        backward = tap < 0
        before = jnp.where(backward & (row > 0), g0, 0.0)
        here = jnp.where(backward, g1, g0)
        after = jnp.where(jnp.logical_not(backward) & (row < rows - 1), g1, 0.0)
        return before, here, after

    def by_lane(level, parity, second):
        pair = [weights(level, child, parity) for child in range(2)]
        return [jnp.where(second, odd, even) for even, odd in zip(*pair)]

    def neighbours(value):
        return pltpu.roll(value, 1, 0), value, pltpu.roll(value, rows - 1, 0)

    def blend(near, weight):
        return near[0] * weight[0] + near[1] * weight[1] + near[2] * weight[2]

    def of_core(value):
        tiles = value.reshape(rows // 16, 2, 8, FA)
        return jnp.where(core == 0, tiles[:, 0], tiles[:, 1]).reshape(rows // 2, FA)

    level2 = [weights(1, child, e2) for child in range(2)]
    level3 = [weights(2, child, e3) for child in range(2)]
    level4 = [of_core(w) for w in by_lane(3, e4, (lane // 8) % 2 == 1)]
    imaginary = lane[: rows // 2] % 2 == 1

    @pl.when(pl.program_id(0) == 0)
    def _():
        for e1 in range(2):
            level1 = by_lane(0, e1, (lane // 4) % 2 == 1)
            for slot in range(2):
                source = jnp.where(slot == 0, core, 1 - core)
                firsts[e1 * 2 + slot] = blend(neighbours(dot(data, mixing[source])), level1)

    @pl.when(e3 == 0)
    def _():
        for at in range(4):
            near = neighbours(firsts[at])
            for c2 in range(2):
                seconds[e2, at * 2 + c2] = blend(near, level2[c2])

    for e1 in range(2):
        for slot, out in ((0, out_own), (1, out_other)):
            for c2 in range(2):
                second = neighbours(seconds[e2, (e1 * 2 + slot) * 2 + c2])
                for c3 in range(2):
                    third = [of_core(v) for v in neighbours(blend(second, level3[c3]))]
                    real_row = blend(third, level4)
                    imag_row = jnp.where(
                        imaginary, pltpu.roll(real_row, 1, 1), -pltpu.roll(real_row, FA - 1, 1)
                    )
                    both = [v.reshape(rows // 16, 8, FA) for v in (real_row, imag_row)]
                    at = (c3 * 2 + c2) * FA
                    out[0, :, e1, :, at : at + FA] = jnp.concatenate(both, axis=1).astype(BF16)


def beam_factors(place, gains, packed, beams, own_pulses):
    rows = packed.shape[0]
    pulses = beams * own_pulses
    chips = beams // 2
    mixing = np.zeros((2, FA, FA), ml_dtypes.bfloat16)
    for core, chip, c4, c1, p, i in np.ndindex(2, chips, 2, 2, own_pulses, 2):
        lane = (((chip * 2 + c4) * 2 + c1) * own_pulses + p) * 2 + i
        mixing[core, i * pulses + (chip * 2 + core) * own_pulses + p, lane] = -1 if i else 1
    shape = jax.ShapeDtypeStruct((4, chips, 2, 16, 4 * FA), BF16)
    spec = pl.BlockSpec((1, chips, 2, 16, 4 * FA), lambda g: (g, 0, 0, 0, 0))
    def kernel(*refs):
        beam_kernel(2 * pulses, *refs)

    return pl.pallas_call(
        kernel,
        grid=(4,),
        out_shape=(shape, shape),
        in_specs=[SMEM, SMEM, VMEM, VMEM],
        out_specs=(spec, spec),
        scratch_shapes=[
            pltpu.VMEM((4, rows, FA), F32),
            pltpu.VMEM((2, 8, rows, FA), F32),
        ],
        compiler_params=pltpu.CompilerParams(vmem_limit_bytes=32 * 2**20),
        cost_estimate=pl.CostEstimate(flops=10**6, bytes_accessed=10**5, transcendentals=0),
    )(place, gains, packed, jnp.asarray(mixing))


def gather_rows(packed, core, chip):
    steps = [("core", 1, core)] + [("chip", 1 << bit, (chip >> bit) & 1) for bit in range(3)]
    for axis, apart, upper in steps:
        size = lax.axis_size(axis)
        got = lax.ppermute(packed, axis, [(i, i ^ apart) for i in range(size)])
        low, high = jnp.where(upper == 0, packed, got), jnp.where(upper == 0, got, packed)
        packed = jnp.concatenate([low, high], axis=0)
    return packed


def local(echoes, matched_filter, steering, kernels, blend_gains, beam_taps):
    zh = lax.axis_index("zh")
    zl = lax.axis_index("zl")
    core = lax.axis_index("core")
    own_rows = steering.shape[1]
    pulses = steering.shape[2]
    own_pulses = echoes.shape[1]
    beams = pulses // own_pulses
    slices = 4 * beams // 2
    place = ((zh * 4 + zl) * 2 + core).astype(jnp.int32).reshape(1)
    tables = [jnp.asarray(table) for table in dft_blocks()]

    message = compress_own(
        place, echoes, matched_filter, kernels, tables, 2, slices
    )
    message, steering, beam_taps = lax.optimization_barrier((message, steering, beam_taps))
    width = message.shape[2]
    own = lax.all_to_all(
        message.reshape(2 * slices, width, -1), ("zl", "chip", "zh"), 0, 0, tiled=True
    ).reshape(2 * slices * width, -1)

    packed = jnp.concatenate(
        [
            jnp.moveaxis(steering, 1, 0).reshape(own_rows, 2 * pulses),
            jnp.moveaxis(beam_taps, 3, 0).reshape(own_rows, 4 * LEVELS).astype(BF16),
        ],
        axis=1,
    )
    packed = jnp.pad(packed, ((0, 0), (0, FA - packed.shape[1])))
    packed = gather_rows(packed, core, lax.axis_index("chip"))
    near, far = beam_factors(place, blend_gains.reshape(-1), packed, beams, own_pulses)

    own, near, far = lax.optimization_barrier((own, near, far))
    other = lax.ppermute(own, "core", [(0, 1), (1, 0)])
    total = dot(near.reshape(-1, 4 * FA), own)
    total = total + dot(far.reshape(-1, 4 * FA), other)
    result = total.astype(BF16).reshape(slices, 4 * own_rows, -1)
    arrived = lax.all_to_all(result, ("zl", "chip"), 0, 0, tiled=True)
    arrived = arrived.reshape(slices, 2, 2, own_rows, -1, FA)
    return jnp.transpose(arrived, (1, 3, 2, 4, 0, 5)).reshape(2, own_rows, 2, -1)


def solution(mesh):
    fine = Mesh(mesh.devices.reshape(4, 2, 4, 8, 2), ("g", "zh", "zl", "chip", "core"))
    sub = ("g", "zh", "zl")
    beam = ("chip", "core")
    return jax.shard_map(
        local,
        mesh=fine,
        in_specs=(
            P(sub, beam, None, None),
            P(),
            P(None, beam, None),
            P(),
            P(),
            P(None, None, None, beam),
        ),
        out_specs=P(sub, beam, None, None),
        check_vma=False,
    )
```

```python
import math

import jax
import jax.numpy as jnp
import ml_dtypes
import numpy as np
from jax import lax
from jax.experimental import pallas as pl
from jax.experimental.pallas import tpu as pltpu
from jax.sharding import Mesh
from jax.sharding import PartitionSpec as P

FA = 128
LEVELS = 4
BF16 = jnp.bfloat16
F32 = jnp.float32


def halves(table):
    high = table.astype(ml_dtypes.bfloat16)
    low = (table - high.astype(np.float64)).astype(ml_dtypes.bfloat16)
    return np.stack([high, low])


def dft_blocks():
    index = np.arange(FA)
    product = index[:, None] * index[None, :]
    angle = (product % FA) * (2.0 * math.pi / FA)
    c, s = np.cos(angle), np.sin(angle)
    turn = (product % (FA * FA)) * (2.0 * math.pi / (FA * FA))
    return (
        halves(np.block([[c, s], [-s, c]])),
        halves(np.block([[c, -s], [s, c]])),
        np.stack([np.cos(turn), np.sin(turn)]).astype(np.float32),
    )


def split(value):
    high = value.astype(BF16)
    return high, (value - high.astype(F32)).astype(BF16)


def dot(left, right):
    return jnp.dot(left, right, preferred_element_type=F32)


def dot_table(value, table):
    high, low = split(value)
    return dot(high, table[0]) + dot(low, table[0]) + dot(high, table[1])


def table_dot(table, value):
    high, low = split(value)
    return dot(table[0], high) + dot(table[0], low) + dot(table[1], high)


def complex_block(ref, *index):
    real_part, imag_part = ref[(*index, 0)], ref[(*index, 1)]
    top = jnp.concatenate([real_part, imag_part], axis=1)
    return jnp.concatenate([top, jnp.concatenate([-imag_part, real_part], axis=1)], axis=0)


def place_bits(place):
    value = place[0]
    return (value >> 1) & 1, (value >> 2) & 1, (value >> 3) & 1, value & 1


def range_matrices(bits, kern):
    chain = complex_block(kern, 3, bits[2]).astype(F32)
    for level in (2, 1):
        high, low = split(chain)
        block = complex_block(kern, level, bits[level - 1])
        chain = dot(block, high) + dot(block, low)
    high, low = split(chain)
    mats = []
    for child in range(2):
        block = complex_block(kern, 0, child)
        mats.append((dot(block, high) + dot(block, low)).astype(BF16))
    return mats


def forward_left(signal, plus, turn):
    count = signal.shape[1] // FA
    c, s = turn[0], turn[1]
    first = dot(plus[0], signal) + dot(plus[1], signal)
    stacked = []
    for q in range(count):
        real_part = first[:FA, q * FA : (q + 1) * FA]
        imag_part = first[FA:, q * FA : (q + 1) * FA]
        stacked.append(
            jnp.concatenate([real_part * c + imag_part * s, imag_part * c - real_part * s], axis=1)
        )
    return jnp.concatenate(stacked, axis=0)


def filtered(spectrum, filters):
    stacked = []
    for q in range(spectrum.shape[0] // FA):
        real_part = spectrum[q * FA : (q + 1) * FA, :FA]
        imag_part = spectrum[q * FA : (q + 1) * FA, FA:]
        stacked.append(
            jnp.concatenate(
                [
                    real_part * filters[0] - imag_part * filters[1],
                    real_part * filters[1] + imag_part * filters[0],
                ],
                axis=1,
            )
        )
    return jnp.concatenate(stacked, axis=0)


def inverse_left(back, minus, turn):
    c, s = turn[0], turn[1]
    stacked = []
    for q in range(back.shape[0] // FA):
        real_part = back[q * FA : (q + 1) * FA, :FA]
        imag_part = back[q * FA : (q + 1) * FA, FA:]
        stacked.append(
            jnp.concatenate([real_part * c - imag_part * s, imag_part * c + real_part * s], axis=0)
        )
    return table_dot(minus, jnp.concatenate(stacked, axis=1)).astype(BF16)


def times_range(pulses, mats, rows):
    count = pulses.shape[1] // FA
    for q in range(count):
        lanes = slice(q * FA, (q + 1) * FA)
        pair = jnp.concatenate([pulses[:FA, lanes], pulses[FA:, lanes]], axis=1)
        turned = dot(pair, mats[q * 2 // count])
        rows[pl.ds(2 * q, FA, stride=2 * count), :] = turned[:, :FA]
        rows[pl.ds(2 * q + 1, FA, stride=2 * count), :] = turned[:, FA:]


def send_order(rows, out):
    slices, copies, width = out.shape[:3]
    for part in range(FA // slices):
        piece = rows[pl.ds(part * slices * width, slices * width), :]
        piece = piece.reshape(slices, width, FA).astype(BF16)
        for copy in range(copies):
            out[:, copy, :, part * FA : (part + 1) * FA] = piece


def own_kernel(place, echo_hbm, matched_hbm, kern_hbm, plus_hbm, minus_hbm, turn_hbm, out, *refs):
    echo, matched, kern, plus, minus, turn, signal, lines, rows, sems = refs
    loads = [
        pltpu.make_async_copy(source, target, sems.at[at])
        for at, (source, target) in enumerate(
            (
                (echo_hbm, echo),
                (plus_hbm, plus),
                (turn_hbm, turn),
                (kern_hbm, kern),
                (minus_hbm, minus),
                (matched_hbm, matched),
            )
        )
    ]
    for load in loads:
        load.start()
    loads[0].wait()
    pulses = echo.shape[1]
    for n in range(FA):
        for q in range(echo.shape[0] * pulses):
            pair = echo[q // pulses, q % pulses, :, n * FA : (n + 1) * FA].astype(F32)
            signal[n : n + 1, q * FA : (q + 1) * FA] = pair[0:1]
            signal[FA + n : FA + n + 1, q * FA : (q + 1) * FA] = pair[1:2]
    for load in loads[1:]:
        load.wait()
    mats = range_matrices(place_bits(place), kern)
    turned = forward_left(signal[...].astype(BF16), plus, turn)
    spectrum = dot_table(turned, minus)
    for j in range(FA):
        lines[0, j : j + 1, :] = matched[0:1, j * FA : (j + 1) * FA]
        lines[1, j : j + 1, :] = matched[1:2, j * FA : (j + 1) * FA]
    scale = 1.0 / (FA * FA)
    filters = [jnp.transpose(lines[part]) * scale for part in range(2)]
    back = dot_table(filtered(spectrum, filters), plus)
    times_range(inverse_left(back, minus, turn), mats, rows)
    send_order(rows, out)


SMEM = pl.BlockSpec(memory_space=pltpu.SMEM)
VMEM = pl.BlockSpec(memory_space=pltpu.VMEM)
ANY = pl.BlockSpec(memory_space=pl.ANY)


def compress_own(place, echo, matched, kern, tables, copies, slices):
    large = [echo, matched, kern, *tables]
    width = 2 * echo.shape[0] * echo.shape[1]
    return pl.pallas_call(
        own_kernel,
        out_shape=jax.ShapeDtypeStruct((slices, copies, width, FA * FA // slices), BF16),
        in_specs=[SMEM] + [ANY] * len(large),
        out_specs=VMEM,
        scratch_shapes=[pltpu.VMEM(table.shape, table.dtype) for table in large]
        + [
            pltpu.VMEM((2 * FA, width // 2 * FA), F32),
            pltpu.VMEM((2, FA, FA), F32),
            pltpu.VMEM((FA * width, FA), F32),
            pltpu.SemaphoreType.DMA((len(large),)),
        ],
        compiler_params=pltpu.CompilerParams(vmem_limit_bytes=60 * 2**20),
        cost_estimate=pl.CostEstimate(flops=10**9, bytes_accessed=2 * 10**6, transcendentals=0),
    )(place, *large)


def beam_kernel(steer_lanes, place, gains, packed, mixing, out_own, out_other, firsts, seconds, lasts):
    e3 = pl.program_id(0) // 2
    e2 = pl.program_id(0) % 2
    _, _, e4, core = place_bits(place)
    rows = packed.shape[0]
    data = packed[...]
    taps = data.astype(F32)
    row = lax.broadcasted_iota(jnp.int32, (rows, FA), 0)
    lane = lax.broadcasted_iota(jnp.int32, (rows, FA), 1)

    def weights(level, child, parity):
        at = steer_lanes + (level * 2 + child) * 2
        even, odd = taps[:, at : at + 1], taps[:, at + 1 : at + 2]
        if isinstance(parity, int):
            tap = odd if parity else even
        else:
            tap = jnp.where(parity == 1, odd, even)
        tap = jnp.broadcast_to(tap, (rows, FA))
        index = ((level * 2 + child) * 2 + parity) * 2
        g0, g1 = gains[index], gains[index + 1]
        backward = tap < 0
        before = jnp.where(backward & (row > 0), g0, 0.0)
        here = jnp.where(backward, g1, g0)
        after = jnp.where(jnp.logical_not(backward) & (row < rows - 1), g1, 0.0)
        return before, here, after

    def by_lane(level, parity, second):
        pair = [weights(level, child, parity) for child in range(2)]
        return [jnp.where(second, odd, even) for even, odd in zip(*pair)]

    def neighbours(value):
        return pltpu.roll(value, 1, 0), value, pltpu.roll(value, rows - 1, 0)

    def blend(near, weight):
        return near[0] * weight[0] + near[1] * weight[1] + near[2] * weight[2]

    def of_core(value):
        tiles = value.reshape(rows // 16, 2, 8, FA)
        return jnp.where(core == 0, tiles[:, 0], tiles[:, 1]).reshape(rows // 2, FA)

    level3 = [weights(2, child, e3) for child in range(2)]
    imaginary = lane[: rows // 2] % 2 == 1

    @pl.when(pl.program_id(0) == 0)
    def _():
        for at, weight in enumerate(by_lane(3, e4, (lane // 8) % 2 == 1)):
            lasts[at] = of_core(weight)
        for e1 in range(2):
            level1 = by_lane(0, e1, (lane // 4) % 2 == 1)
            for slot in range(2):
                source = jnp.where(slot == 0, core, 1 - core)
                firsts[e1 * 2 + slot] = blend(neighbours(dot(data, mixing[source])), level1)

    @pl.when(e3 == 0)
    def _():
        level2 = [weights(1, child, e2) for child in range(2)]
        for at in range(4):
            near = neighbours(firsts[at])
            for c2 in range(2):
                seconds[e2, at * 2 + c2] = blend(near, level2[c2])

    level4 = [lasts[at] for at in range(3)]
    for e1 in range(2):
        for slot, out in ((0, out_own), (1, out_other)):
            for c2 in range(2):
                second = neighbours(seconds[e2, (e1 * 2 + slot) * 2 + c2])
                for c3 in range(2):
                    third = [of_core(v) for v in neighbours(blend(second, level3[c3]))]
                    real_row = blend(third, level4)
                    imag_row = jnp.where(
                        imaginary, pltpu.roll(real_row, 1, 1), -pltpu.roll(real_row, FA - 1, 1)
                    )
                    both = [v.reshape(rows // 16, 8, FA) for v in (real_row, imag_row)]
                    at = (c3 * 2 + c2) * FA
                    out[0, :, e1, :, at : at + FA] = jnp.concatenate(both, axis=1).astype(BF16)


def beam_factors(place, gains, packed, beams, own_pulses):
    rows = packed.shape[0]
    pulses = beams * own_pulses
    chips = beams // 2
    mixing = np.zeros((2, FA, FA), ml_dtypes.bfloat16)
    for core, chip, c4, c1, p, i in np.ndindex(2, chips, 2, 2, own_pulses, 2):
        lane = (((chip * 2 + c4) * 2 + c1) * own_pulses + p) * 2 + i
        mixing[core, i * pulses + (chip * 2 + core) * own_pulses + p, lane] = -1 if i else 1
    shape = jax.ShapeDtypeStruct((4, chips, 2, 16, 4 * FA), BF16)
    spec = pl.BlockSpec((1, chips, 2, 16, 4 * FA), lambda g: (g, 0, 0, 0, 0))
    def kernel(*refs):
        beam_kernel(2 * pulses, *refs)

    return pl.pallas_call(
        kernel,
        grid=(4,),
        out_shape=(shape, shape),
        in_specs=[SMEM, SMEM, VMEM, VMEM],
        out_specs=(spec, spec),
        scratch_shapes=[
            pltpu.VMEM((4, rows, FA), F32),
            pltpu.VMEM((2, 8, rows, FA), F32),
            pltpu.VMEM((3, rows // 2, FA), F32),
        ],
        compiler_params=pltpu.CompilerParams(vmem_limit_bytes=32 * 2**20),
        cost_estimate=pl.CostEstimate(flops=10**6, bytes_accessed=10**5, transcendentals=0),
    )(place, gains, packed, jnp.asarray(mixing))


def gather_rows(packed, core, chip):
    steps = [("core", 1, core)] + [("chip", 1 << bit, (chip >> bit) & 1) for bit in range(3)]
    for axis, apart, upper in steps:
        size = lax.axis_size(axis)
        got = lax.ppermute(packed, axis, [(i, i ^ apart) for i in range(size)])
        low, high = jnp.where(upper == 0, packed, got), jnp.where(upper == 0, got, packed)
        packed = jnp.concatenate([low, high], axis=0)
    return packed


def local(echoes, matched_filter, steering, kernels, blend_gains, beam_taps):
    zh = lax.axis_index("zh")
    zl = lax.axis_index("zl")
    core = lax.axis_index("core")
    own_rows = steering.shape[1]
    pulses = steering.shape[2]
    own_pulses = echoes.shape[1]
    beams = pulses // own_pulses
    slices = 4 * beams // 2
    place = ((zh * 4 + zl) * 2 + core).astype(jnp.int32).reshape(1)
    tables = [jnp.asarray(table) for table in dft_blocks()]

    message = compress_own(
        place, echoes, matched_filter, kernels, tables, 2, slices
    )
    message, steering, beam_taps = lax.optimization_barrier((message, steering, beam_taps))
    width = message.shape[2]
    own = lax.all_to_all(
        message.reshape(2 * slices, width, -1), ("zl", "chip", "zh"), 0, 0, tiled=True
    ).reshape(2 * slices * width, -1)

    packed = jnp.concatenate(
        [
            jnp.moveaxis(steering, 1, 0).reshape(own_rows, 2 * pulses),
            jnp.moveaxis(beam_taps, 3, 0).reshape(own_rows, 4 * LEVELS).astype(BF16),
        ],
        axis=1,
    )
    packed = jnp.pad(packed, ((0, 0), (0, FA - packed.shape[1])))
    packed = gather_rows(packed, core, lax.axis_index("chip"))
    near, far = beam_factors(place, blend_gains.reshape(-1), packed, beams, own_pulses)

    own, near, far = lax.optimization_barrier((own, near, far))
    other = lax.ppermute(own, "core", [(0, 1), (1, 0)])
    total = dot(near.reshape(-1, 4 * FA), own)
    total = total + dot(far.reshape(-1, 4 * FA), other)
    result = total.astype(BF16).reshape(slices, 4 * own_rows, -1)
    arrived = lax.all_to_all(result, ("zl", "chip"), 0, 0, tiled=True)
    arrived = arrived.reshape(slices, 2, 2, own_rows, -1, FA)
    return jnp.transpose(arrived, (1, 3, 2, 4, 0, 5)).reshape(2, own_rows, 2, -1)


def solution(mesh):
    fine = Mesh(mesh.devices.reshape(4, 2, 4, 8, 2), ("g", "zh", "zl", "chip", "core"))
    sub = ("g", "zh", "zl")
    beam = ("chip", "core")
    return jax.shard_map(
        local,
        mesh=fine,
        in_specs=(
            P(sub, beam, None, None),
            P(),
            P(None, beam, None),
            P(),
            P(),
            P(None, None, None, beam),
        ),
        out_specs=P(sub, beam, None, None),
        check_vma=False,
    )
```

```python
import math

import jax
import jax.numpy as jnp
import ml_dtypes
import numpy as np
from jax import lax
from jax.experimental import pallas as pl
from jax.experimental.pallas import tpu as pltpu
from jax.sharding import Mesh
from jax.sharding import PartitionSpec as P

FA = 128
LEVELS = 4
BF16 = jnp.bfloat16
F32 = jnp.float32


def halves(table):
    high = table.astype(ml_dtypes.bfloat16)
    low = (table - high.astype(np.float64)).astype(ml_dtypes.bfloat16)
    return np.stack([high, low])


def dft_blocks():
    index = np.arange(FA)
    product = index[:, None] * index[None, :]
    angle = (product % FA) * (2.0 * math.pi / FA)
    c, s = np.cos(angle), np.sin(angle)
    turn = (product % (FA * FA)) * (2.0 * math.pi / (FA * FA))
    return (
        halves(np.block([[c, s], [-s, c]])),
        halves(np.block([[c, -s], [s, c]])),
        np.stack([np.cos(turn), np.sin(turn)]).astype(np.float32),
    )


def split(value):
    high = value.astype(BF16)
    return high, (value - high.astype(F32)).astype(BF16)


def dot(left, right):
    return jnp.dot(left, right, preferred_element_type=F32)


def dot_table(value, table):
    high, low = split(value)
    return dot(high, table[0]) + dot(low, table[0]) + dot(high, table[1])


def table_dot(table, value):
    high, low = split(value)
    return dot(table[0], high) + dot(table[0], low) + dot(table[1], high)


def complex_block(ref, *index):
    real_part, imag_part = ref[(*index, 0)], ref[(*index, 1)]
    top = jnp.concatenate([real_part, imag_part], axis=1)
    return jnp.concatenate([top, jnp.concatenate([-imag_part, real_part], axis=1)], axis=0)


def place_bits(place):
    value = place[0]
    return (value >> 1) & 1, (value >> 2) & 1, (value >> 3) & 1, value & 1


def range_matrices(bits, kern):
    chain = complex_block(kern, 3, bits[2]).astype(F32)
    for level in (2, 1):
        high, low = split(chain)
        block = complex_block(kern, level, bits[level - 1])
        chain = dot(block, high) + dot(block, low)
    high, low = split(chain)
    mats = []
    for child in range(2):
        block = complex_block(kern, 0, child)
        mats.append((dot(block, high) + dot(block, low)).astype(BF16))
    return mats


def forward_left(signal, plus, turn):
    count = signal.shape[1] // FA
    c, s = turn[0], turn[1]
    first = dot(plus[0], signal) + dot(plus[1], signal)
    stacked = []
    for q in range(count):
        real_part = first[:FA, q * FA : (q + 1) * FA]
        imag_part = first[FA:, q * FA : (q + 1) * FA]
        stacked.append(
            jnp.concatenate([real_part * c + imag_part * s, imag_part * c - real_part * s], axis=1)
        )
    return jnp.concatenate(stacked, axis=0)


def filtered(spectrum, filters):
    stacked = []
    for q in range(spectrum.shape[0] // FA):
        real_part = spectrum[q * FA : (q + 1) * FA, :FA]
        imag_part = spectrum[q * FA : (q + 1) * FA, FA:]
        stacked.append(
            jnp.concatenate(
                [
                    real_part * filters[0] - imag_part * filters[1],
                    real_part * filters[1] + imag_part * filters[0],
                ],
                axis=1,
            )
        )
    return jnp.concatenate(stacked, axis=0)


def inverse_left(back, minus, turn):
    c, s = turn[0], turn[1]
    stacked = []
    for q in range(back.shape[0] // FA):
        real_part = back[q * FA : (q + 1) * FA, :FA]
        imag_part = back[q * FA : (q + 1) * FA, FA:]
        stacked.append(
            jnp.concatenate([real_part * c - imag_part * s, imag_part * c + real_part * s], axis=0)
        )
    return table_dot(minus, jnp.concatenate(stacked, axis=1)).astype(BF16)


def times_range(pulses, mats, rows):
    count = pulses.shape[1] // FA
    for q in range(count):
        lanes = slice(q * FA, (q + 1) * FA)
        pair = jnp.concatenate([pulses[:FA, lanes], pulses[FA:, lanes]], axis=1)
        turned = dot(pair, mats[q * 2 // count])
        rows[pl.ds(2 * q, FA, stride=2 * count), :] = turned[:, :FA]
        rows[pl.ds(2 * q + 1, FA, stride=2 * count), :] = turned[:, FA:]


def send_order(rows, out):
    slices, copies, width = out.shape[:3]
    for part in range(FA // slices):
        piece = rows[pl.ds(part * slices * width, slices * width), :]
        piece = piece.reshape(slices, width, FA).astype(BF16)
        for copy in range(copies):
            out[:, copy, :, part * FA : (part + 1) * FA] = piece


def own_kernel(place, echo_hbm, matched_hbm, kern_hbm, plus_hbm, minus_hbm, turn_hbm, out, *refs):
    echo, matched, kern, plus, minus, turn, signal, lines, rows, sems = refs
    loads = [
        pltpu.make_async_copy(source, target, sems.at[at])
        for at, (source, target) in enumerate(
            (
                (echo_hbm, echo),
                (plus_hbm, plus),
                (turn_hbm, turn),
                (kern_hbm, kern),
                (minus_hbm, minus),
                (matched_hbm, matched),
            )
        )
    ]
    for load in loads:
        load.start()
    loads[0].wait()
    pulses = echo.shape[1]
    for n in range(FA):
        for q in range(echo.shape[0] * pulses):
            pair = echo[q // pulses, q % pulses, :, n * FA : (n + 1) * FA].astype(F32)
            signal[n : n + 1, q * FA : (q + 1) * FA] = pair[0:1]
            signal[FA + n : FA + n + 1, q * FA : (q + 1) * FA] = pair[1:2]
    for load in loads[1:]:
        load.wait()
    mats = range_matrices(place_bits(place), kern)
    turned = forward_left(signal[...].astype(BF16), plus, turn)
    spectrum = dot_table(turned, minus)
    for j in range(FA):
        lines[0, j : j + 1, :] = matched[0:1, j * FA : (j + 1) * FA]
        lines[1, j : j + 1, :] = matched[1:2, j * FA : (j + 1) * FA]
    scale = 1.0 / (FA * FA)
    filters = [jnp.transpose(lines[part]) * scale for part in range(2)]
    back = dot_table(filtered(spectrum, filters), plus)
    times_range(inverse_left(back, minus, turn), mats, rows)
    send_order(rows, out)


SMEM = pl.BlockSpec(memory_space=pltpu.SMEM)
VMEM = pl.BlockSpec(memory_space=pltpu.VMEM)
ANY = pl.BlockSpec(memory_space=pl.ANY)


def compress_own(place, echo, matched, kern, tables, copies, slices):
    large = [echo, matched, kern, *tables]
    width = 2 * echo.shape[0] * echo.shape[1]
    return pl.pallas_call(
        own_kernel,
        out_shape=jax.ShapeDtypeStruct((slices, copies, width, FA * FA // slices), BF16),
        in_specs=[SMEM] + [ANY] * len(large),
        out_specs=VMEM,
        scratch_shapes=[pltpu.VMEM(table.shape, table.dtype) for table in large]
        + [
            pltpu.VMEM((2 * FA, width // 2 * FA), F32),
            pltpu.VMEM((2, FA, FA), F32),
            pltpu.VMEM((FA * width, FA), F32),
            pltpu.SemaphoreType.DMA((len(large),)),
        ],
        compiler_params=pltpu.CompilerParams(vmem_limit_bytes=60 * 2**20),
        cost_estimate=pl.CostEstimate(flops=10**9, bytes_accessed=2 * 10**6, transcendentals=0),
    )(place, *large)


def beam_kernel(steer_lanes, place, gains, packed, mixing, out_own, out_other, firsts, seconds, lasts, thirds):
    e3 = pl.program_id(0) // 2
    e2 = pl.program_id(0) % 2
    _, _, e4, core = place_bits(place)
    rows = packed.shape[0]
    data = packed[...]
    taps = data.astype(F32)
    row = lax.broadcasted_iota(jnp.int32, (rows, FA), 0)
    lane = lax.broadcasted_iota(jnp.int32, (rows, FA), 1)

    def weights(level, child, parity):
        at = steer_lanes + (level * 2 + child) * 2
        even, odd = taps[:, at : at + 1], taps[:, at + 1 : at + 2]
        if isinstance(parity, int):
            tap = odd if parity else even
        else:
            tap = jnp.where(parity == 1, odd, even)
        tap = jnp.broadcast_to(tap, (rows, FA))
        index = ((level * 2 + child) * 2 + parity) * 2
        g0, g1 = gains[index], gains[index + 1]
        backward = tap < 0
        before = jnp.where(backward & (row > 0), g0, 0.0)
        here = jnp.where(backward, g1, g0)
        after = jnp.where(jnp.logical_not(backward) & (row < rows - 1), g1, 0.0)
        return before, here, after

    def by_lane(level, parity, second):
        pair = [weights(level, child, parity) for child in range(2)]
        return [jnp.where(second, odd, even) for even, odd in zip(*pair)]

    def neighbours(value):
        return pltpu.roll(value, 1, 0), value, pltpu.roll(value, rows - 1, 0)

    def blend(near, weight):
        return near[0] * weight[0] + near[1] * weight[1] + near[2] * weight[2]

    def of_core(value):
        tiles = value.reshape(rows // 16, 2, 8, FA)
        return jnp.where(core == 0, tiles[:, 0], tiles[:, 1]).reshape(rows // 2, FA)


    @pl.when(e2 == 0)
    def _():
        for child in range(2):
            for at, weight in enumerate(weights(2, child, e3)):
                thirds[child, at] = weight

    imaginary = lane[: rows // 2] % 2 == 1

    @pl.when(pl.program_id(0) == 0)
    def _():
        for at, weight in enumerate(by_lane(3, e4, (lane // 8) % 2 == 1)):
            lasts[at] = of_core(weight)
        for e1 in range(2):
            level1 = by_lane(0, e1, (lane // 4) % 2 == 1)
            for slot in range(2):
                source = jnp.where(slot == 0, core, 1 - core)
                firsts[e1 * 2 + slot] = blend(neighbours(dot(data, mixing[source])), level1)

    @pl.when(e3 == 0)
    def _():
        level2 = [weights(1, child, e2) for child in range(2)]
        for at in range(4):
            near = neighbours(firsts[at])
            for c2 in range(2):
                seconds[e2, at * 2 + c2] = blend(near, level2[c2])

    level3 = [[thirds[child, at] for at in range(3)] for child in range(2)]
    level4 = [lasts[at] for at in range(3)]
    for e1 in range(2):
        for slot, out in ((0, out_own), (1, out_other)):
            for c2 in range(2):
                second = neighbours(seconds[e2, (e1 * 2 + slot) * 2 + c2])
                for c3 in range(2):
                    third = [of_core(v) for v in neighbours(blend(second, level3[c3]))]
                    real_row = blend(third, level4)
                    imag_row = jnp.where(
                        imaginary, pltpu.roll(real_row, 1, 1), -pltpu.roll(real_row, FA - 1, 1)
                    )
                    both = [v.reshape(rows // 16, 8, FA) for v in (real_row, imag_row)]
                    at = (c3 * 2 + c2) * FA
                    out[0, :, e1, :, at : at + FA] = jnp.concatenate(both, axis=1).astype(BF16)


def beam_factors(place, gains, packed, beams, own_pulses):
    rows = packed.shape[0]
    pulses = beams * own_pulses
    chips = beams // 2
    mixing = np.zeros((2, FA, FA), ml_dtypes.bfloat16)
    for core, chip, c4, c1, p, i in np.ndindex(2, chips, 2, 2, own_pulses, 2):
        lane = (((chip * 2 + c4) * 2 + c1) * own_pulses + p) * 2 + i
        mixing[core, i * pulses + (chip * 2 + core) * own_pulses + p, lane] = -1 if i else 1
    shape = jax.ShapeDtypeStruct((4, chips, 2, 16, 4 * FA), BF16)
    spec = pl.BlockSpec((1, chips, 2, 16, 4 * FA), lambda g: (g, 0, 0, 0, 0))
    def kernel(*refs):
        beam_kernel(2 * pulses, *refs)

    return pl.pallas_call(
        kernel,
        grid=(4,),
        out_shape=(shape, shape),
        in_specs=[SMEM, SMEM, VMEM, VMEM],
        out_specs=(spec, spec),
        scratch_shapes=[
            pltpu.VMEM((4, rows, FA), F32),
            pltpu.VMEM((2, 8, rows, FA), F32),
            pltpu.VMEM((3, rows // 2, FA), F32),
            pltpu.VMEM((2, 3, rows, FA), F32),
        ],
        compiler_params=pltpu.CompilerParams(vmem_limit_bytes=32 * 2**20),
        cost_estimate=pl.CostEstimate(flops=10**6, bytes_accessed=10**5, transcendentals=0),
    )(place, gains, packed, jnp.asarray(mixing))


def gather_rows(packed, core, chip):
    steps = [("core", 1, core)] + [("chip", 1 << bit, (chip >> bit) & 1) for bit in range(3)]
    for axis, apart, upper in steps:
        size = lax.axis_size(axis)
        got = lax.ppermute(packed, axis, [(i, i ^ apart) for i in range(size)])
        low, high = jnp.where(upper == 0, packed, got), jnp.where(upper == 0, got, packed)
        packed = jnp.concatenate([low, high], axis=0)
    return packed


def local(echoes, matched_filter, steering, kernels, blend_gains, beam_taps):
    zh = lax.axis_index("zh")
    zl = lax.axis_index("zl")
    core = lax.axis_index("core")
    own_rows = steering.shape[1]
    pulses = steering.shape[2]
    own_pulses = echoes.shape[1]
    beams = pulses // own_pulses
    slices = 4 * beams // 2
    place = ((zh * 4 + zl) * 2 + core).astype(jnp.int32).reshape(1)
    tables = [jnp.asarray(table) for table in dft_blocks()]

    message = compress_own(
        place, echoes, matched_filter, kernels, tables, 2, slices
    )
    message, steering, beam_taps = lax.optimization_barrier((message, steering, beam_taps))
    width = message.shape[2]
    own = lax.all_to_all(
        message.reshape(2 * slices, width, -1), ("zl", "chip", "zh"), 0, 0, tiled=True
    ).reshape(2 * slices * width, -1)

    packed = jnp.concatenate(
        [
            jnp.moveaxis(steering, 1, 0).reshape(own_rows, 2 * pulses),
            jnp.moveaxis(beam_taps, 3, 0).reshape(own_rows, 4 * LEVELS).astype(BF16),
        ],
        axis=1,
    )
    packed = jnp.pad(packed, ((0, 0), (0, FA - packed.shape[1])))
    packed = gather_rows(packed, core, lax.axis_index("chip"))
    near, far = beam_factors(place, blend_gains.reshape(-1), packed, beams, own_pulses)

    own, near, far = lax.optimization_barrier((own, near, far))
    other = lax.ppermute(own, "core", [(0, 1), (1, 0)])
    total = dot(near.reshape(-1, 4 * FA), own)
    total = total + dot(far.reshape(-1, 4 * FA), other)
    result = total.astype(BF16).reshape(slices, 4 * own_rows, -1)
    arrived = lax.all_to_all(result, ("zl", "chip"), 0, 0, tiled=True)
    arrived = arrived.reshape(slices, 2, 2, own_rows, -1, FA)
    return jnp.transpose(arrived, (1, 3, 2, 4, 0, 5)).reshape(2, own_rows, 2, -1)


def solution(mesh):
    fine = Mesh(mesh.devices.reshape(4, 2, 4, 8, 2), ("g", "zh", "zl", "chip", "core"))
    sub = ("g", "zh", "zl")
    beam = ("chip", "core")
    return jax.shard_map(
        local,
        mesh=fine,
        in_specs=(
            P(sub, beam, None, None),
            P(),
            P(None, beam, None),
            P(),
            P(),
            P(None, None, None, beam),
        ),
        out_specs=P(sub, beam, None, None),
        check_vma=False,
    )
```
